256 devices in a mesh: ctx: 32 (over y, z), fsdp: 8 (over x, core).
Axes of the slice: x: 4, y: 4, z: 8, core: 2. Of those that a mesh axis runs over, the one named last changes fastest.
Arguments:
- tokens: int32 [16384], P('ctx'), may hold values from 0 to 511
- embedding: bfloat16 [512, 4096], P(None, 'fsdp'), may hold values from -6 to 6
- norm_gain: float32 [4096], replicated, may hold values from 0.1 to 1.9
- in_weight: bfloat16 [4096, 3, 2048], P('ctx', None, 'fsdp'), may hold values from -0.09375 to 0.09375
- short_taps: float32 [7, 3, 2048], P(None, None, 'fsdp'), may hold values from -2 to 2
- decay_rates: float32 [16, 128], P(None, 'fsdp'), may hold values from 3.0517578e-05 to 0.1
- residue: float32 [16, 128], P(None, 'fsdp'), may hold values from -0.078125 to 0.078125
- skip_weight: float32 [2048], P('fsdp'), may hold values from -4 to 4
- out_weight: bfloat16 [2048, 4096], P('fsdp', 'ctx'), may hold values from -0.125 to 0.125
Outputs:
- mixed: bfloat16 [16384, 4096], P('ctx', 'fsdp')
The draws below stay inside these ranges and needn't reach their ends.
All inputs are finite; a program needn't handle non-finite values.
Results may differ from the reference program's by a relative error of at most 0.018.
Values may be sent and summed in bfloat16 or wider, within the bound.
A program may use at most 64 MiB of HBM per device.

```python
import math
import jax
import jax.numpy as jnp
import numpy as np
from jax import lax

D = 4096
VOCAB = 512
C = 2048
GROUP = 16
MODES = 16
TAPS = 7
SEQ = 16384
GROUPS = 128


def set_ends(drawn, rng, least, largest):
    longest = drawn.shape.index(max(drawn.shape))
    spots = []
    for shift in (0, 1):
        where = [jax.random.randint(jax.random.fold_in(rng, axis), (), 0, length) for axis, length in enumerate(drawn.shape)]
        where[longest] = (where[longest] + shift) % drawn.shape[longest]
        spots.append(tuple(where))
    return drawn.at[spots[0]].set(least).at[spots[1]].set(largest)


def block_scale(stream_key, shape, split, smallest, high):
    level = 1.0
    for axis_at, parts in split:
        heights = jax.random.uniform(jax.random.fold_in(jax.random.fold_in(stream_key, 6), axis_at), (parts,), jnp.float32, smallest / len(split), high / len(split))
        level = level * jnp.repeat(jnp.exp(heights), shape[axis_at] // parts).reshape((-1,) + (1,) * (len(shape) - 1 - axis_at))
    return level


def rank_bounds(number_of, skew):
    loads = [(1 << 20) // math.isqrt(grade ** skew) + 1 for grade in range(1, number_of + 1)]
    scale = 1 + sum(loads) // (1 << 30)
    return np.cumsum(np.array([max(1, weight // scale) for weight in loads]))


def ranked(rng, extent, amount, skew):
    table = rank_bounds(amount, skew)
    pick = jax.random.randint(jax.random.fold_in(rng, 1), extent, 0, int(table[amount - 1]))
    rank = jnp.searchsorted(jnp.asarray(table, jnp.int32), pick, side="right")
    return jax.random.permutation(jax.random.fold_in(rng, 2), amount)[rank].astype(jnp.int32)


def gaussian(stream_key, dims, deviation, most, split=(), kind=jnp.bfloat16):
    level = block_scale(stream_key, dims, split, -0.22, 0.18) if split else 1.0
    result = jax.random.normal(stream_key, dims, jnp.float32) * deviation * level
    return jnp.minimum(jnp.maximum(result, -most), most).astype(kind)


def setup_inputs(seed: int = 0) -> dict:
    seeds = jax.random.split(jax.random.key(seed), 10)
    tokens = set_ends(ranked(seeds[0], (SEQ,), VOCAB, 2), jax.random.fold_in(seeds[0], 3), 0, VOCAB - 1).astype(jnp.int32)
    embedding = gaussian(seeds[1], (VOCAB, D), 1.0, 6.0, ((1, 8),))
    norm_gain = jnp.clip(1.0 + 0.18 * jax.random.normal(seeds[2], (D,), jnp.float32), 0.1, 1.9)
    in_weight = gaussian(seeds[3], (D, 3, C), D ** -0.5, 0.09375, ((0, 32), (2, 8)))
    short_taps = gaussian(seeds[4], (TAPS, 3, C), TAPS ** -0.5, 2.0, ((2, 8),), jnp.float32)
    decay_rates = jnp.clip(jnp.exp(math.log(0.1) - 8.094623 * jax.random.uniform(seeds[5], (MODES, GROUPS), jnp.float32) ** block_scale(seeds[5], (MODES, GROUPS), ((1, 8),), -0.2, 0.2)), 3.0517578125e-05, 0.1)
    residue = gaussian(seeds[6], (MODES, GROUPS), ((0.5 / SEQ) ** 0.5), 0.078125, ((1, 8),), jnp.float32)
    skip_weight = gaussian(seeds[7], (C,), 1.0, 4.0, ((0, 8),), jnp.float32)
    out_weight = gaussian(seeds[8], (C, D), C ** -0.5, 0.125, ((0, 8), (1, 32)))
    return dict(tokens=tokens, embedding=embedding, norm_gain=norm_gain, in_weight=in_weight, short_taps=short_taps, decay_rates=decay_rates, residue=residue, skip_weight=skip_weight, out_weight=out_weight)


def reference(tokens, embedding, norm_gain, in_weight, short_taps, decay_rates, residue, skip_weight, out_weight):
    features = jnp.take(embedding, tokens, axis=0)
    widened = features.astype(jnp.float32)
    mean_square = lax.optimization_barrier(jnp.mean(widened * widened, axis=1, keepdims=True))
    normed = (widened * lax.rsqrt(mean_square + 1e-05) * norm_gain).astype(jnp.bfloat16)
    projected = jnp.dot(normed, in_weight.reshape(D, 3 * C), preferred_element_type=jnp.float32)
    projected = projected.reshape(SEQ, 3, C).astype(jnp.bfloat16)
    reach_back = TAPS - 1
    extended = jnp.concatenate([jnp.zeros((reach_back, 3, C), jnp.bfloat16), projected], axis=0).astype(jnp.float32)
    short = jnp.zeros((SEQ, 3, C), jnp.float32)
    for lag_step in range(TAPS):
        short = short + short_taps[lag_step] * extended[reach_back - lag_step:reach_back - lag_step + SEQ]
    queries = short[:, 0, :]
    driving = short[:, 1, :] * short[:, 2, :]
    lag_grid = jnp.arange(SEQ, dtype=jnp.float32)
    filters = lax.optimization_barrier(jnp.sum(residue[None, :, :] * jnp.exp(-decay_rates[None, :, :] * lag_grid[:, None, None]), axis=1))
    filter_spec = jnp.fft.rfft(filters, n=2 * SEQ, axis=0)
    drive_spec = jnp.fft.rfft(driving, n=2 * SEQ, axis=0)
    full_spec = jnp.repeat(filter_spec, GROUP, axis=1)
    convolved = jnp.fft.irfft(drive_spec * full_spec, n=2 * SEQ, axis=0)[:SEQ]
    response = convolved + skip_weight * driving
    gated = (queries * response).astype(jnp.bfloat16)
    return jnp.dot(gated, out_weight, preferred_element_type=jnp.float32).astype(jnp.bfloat16)
```

```python
import jax
import jax.numpy as jnp
from jax import lax
from jax.sharding import PartitionSpec as P

GROUP = 16
CHUNK = 128


def body(
    tokens,
    embedding,
    norm_gain,
    in_weight,
    short_taps,
    decay_rates,
    residue,
    skip_weight,
    out_weight,
):
    count = tokens.shape[0]
    vocab = embedding.shape[0]
    rows = in_weight.shape[0]
    channels = in_weight.shape[2]
    width = norm_gain.shape[0]
    own = lax.axis_index("ctx")
    column = lax.axis_index("fsdp")
    ctx_count = lax.axis_size("ctx")
    fsdp_count = lax.axis_size("fsdp")
    share = ctx_count // fsdp_count

    route = [
        (i * fsdp_count + j, (share * j + i % share) * fsdp_count + i // share)
        for i in range(ctx_count)
        for j in range(fsdp_count)
    ]
    swapped = lax.ppermute(out_weight, ("ctx", "fsdp"), route)
    out_blocks = lax.all_gather(swapped, "ctx", axis=0)
    out_panel = (
        out_blocks.reshape(fsdp_count, share, channels, rows)
        .transpose(0, 2, 1, 3)
        .reshape(fsdp_count * channels, share * rows)
    )

    piece = lax.dynamic_slice(embedding, (0, own % share * rows), (vocab, rows))
    piece = jnp.where(column == own // share, piece, jnp.zeros_like(piece))
    piece = lax.psum(piece, "fsdp").astype(jnp.float32)
    gain = lax.dynamic_slice(norm_gain, (own * rows,), (rows,))
    squares = lax.psum(jnp.sum(piece * piece, axis=1), "ctx")
    scale = lax.rsqrt(squares / width + 1e-05)
    panel = in_weight.reshape(rows, 3 * channels)
    partial_table = jnp.dot(
        (piece * gain).astype(jnp.bfloat16), panel, preferred_element_type=jnp.float32
    ).astype(jnp.bfloat16)
    table = lax.psum_scatter(partial_table, "ctx", scatter_dimension=0, tiled=True)
    table = lax.all_gather(table, "ctx", axis=0, tiled=True)
    table = (table.astype(jnp.float32) * scale[:, None]).astype(jnp.bfloat16)

    reach = short_taps.shape[0] - 1
    before = lax.ppermute(
        tokens[count - reach :], "ctx", [(k, k + 1) for k in range(ctx_count - 1)]
    )
    before = jnp.where(own > 0, before, -1)
    wanted = jnp.concatenate([before, tokens])
    one_hot = (wanted[:, None] == jnp.arange(vocab)[None, :]).astype(jnp.bfloat16)
    projected = jnp.dot(one_hot, table, preferred_element_type=jnp.float32)
    taps = short_taps.reshape(reach + 1, 3 * channels)
    short = jnp.zeros((count, 3 * channels), jnp.float32)
    for lag in range(reach + 1):
        short = short + taps[lag] * projected[reach - lag : reach - lag + count]
    short = short.T
    queries = short[:channels]
    driving = short[channels : 2 * channels] * short[2 * channels :]

    groups = channels // GROUP
    chunks = count // CHUNK
    high = lax.Precision.HIGHEST
    steps = jnp.arange(CHUNK, dtype=jnp.float32)
    lag_grid = steps[None, :] - steps[:, None]
    rates = decay_rates.T
    filters = jnp.sum(
        residue.T[:, :, None] * jnp.exp(-rates[:, :, None] * steps), axis=1
    )
    index = jnp.maximum(lag_grid, 0).astype(jnp.int32)
    toeplitz = jnp.where(lag_grid >= 0, jnp.take(filters, index, axis=1), 0.0)
    blocks = driving.reshape(groups, GROUP, chunks, CHUNK)
    inside = jnp.einsum("gcks,gst->gckt", blocks, toeplitz, precision=high)
    to_end = jnp.exp(-rates[:, :, None] * (CHUNK - 1 - steps))
    ends = jnp.einsum("gcks,gms->kgcm", blocks, to_end, precision=high)
    over_chunk = jnp.exp(-rates * CHUNK)[:, None, :]
    total = ends[0]
    for k in range(1, chunks):
        total = over_chunk * total + ends[k]
    totals = lax.all_gather(total, "ctx", axis=0)
    distance = (own - 1 - jnp.arange(ctx_count)).astype(jnp.float32)
    carried = jnp.where(
        distance[:, None, None] >= 0,
        jnp.exp(-rates[None] * count * jnp.maximum(distance, 0)[:, None, None]),
        0.0,
    )
    state = jnp.sum(carried[:, :, None, :] * totals, axis=0)
    states = [state]
    for k in range(1, chunks):
        states.append(over_chunk * states[-1] + ends[k - 1])
    from_end = residue.T[:, :, None] * jnp.exp(-rates[:, :, None] * (steps + 1))
    outside = jnp.einsum("kgcm,gmt->gckt", jnp.stack(states), from_end, precision=high)
    convolved = (inside + outside).reshape(channels, count)
    response = convolved + skip_weight[:, None] * driving
    gated = (queries * response).astype(jnp.bfloat16).T
    every = lax.all_gather(gated, "fsdp", axis=1, tiled=True)
    return jnp.dot(every, out_panel, preferred_element_type=jnp.float32).astype(
        jnp.bfloat16
    )


def solution(mesh):
    placed = (
        P("ctx"),
        P(None, "fsdp"),
        P(),
        P("ctx", None, "fsdp"),
        P(None, None, "fsdp"),
        P(None, "fsdp"),
        P(None, "fsdp"),
        P("fsdp"),
        P("fsdp", "ctx"),
    )
    return jax.shard_map(
        body, mesh=mesh, in_specs=placed, out_specs=P("ctx", "fsdp"), check_vma=False
    )
```

```python
import functools

import jax
import jax.numpy as jnp
from jax import lax
from jax.experimental import pallas as pl
from jax.experimental.pallas import tpu as pltpu
from jax.sharding import PartitionSpec as P

GROUP = 16
CHUNK = 128
NY, NZ, NX, NC = 4, 8, 4, 2
f32 = jnp.float32
bf16 = jnp.bfloat16
MESH = pl.DeviceIdType.MESH


def split(value):
    high = value.astype(bf16)
    return high, (value - high.astype(f32)).astype(bf16)


def dot(a, b):
    return jnp.dot(a, b, preferred_element_type=f32)


def dot_three(a, b):
    a_high, a_low = split(a)
    b_high, b_low = split(b)
    return dot(a_high, b_high) + dot(a_low, b_high) + dot(a_high, b_low)


def dot_nt(a, b):
    return lax.dot_general(a, b, (((1,), (1,)), ((), ())), preferred_element_type=f32)


def aligned(index, size):
    return pl.multiple_of(index * size, size)


def kernel(
    tokens_ref,
    gain_ref,
    cols_ref,
    rate_row_ref,
    modes_ref,
    wt_ref,
    emb_ref,
    ow_ref,
    out_ref,
    before,
    ebuf,
    enorm,
    wbuf,
    squares,
    partial,
    partial16,
    arrived,
    table,
    one_hot,
    proj,
    driving,
    conv,
    queries,
    toep_high,
    toep_low,
    to_end,
    from_end,
    zstate,
    ystate,
    ends,
    gated_t,
    gated,
    wo,
    total,
    send_sems,
    recv_sems,
):
    i = lax.axis_index("ctx")
    j = lax.axis_index("fsdp")
    y, z = i // NZ, i % NZ
    x, c = j // NC, j % NC
    up, down = (y + 1) % NY, (y + NY - 1) % NY
    opposite = (y + 2) % NY
    right, left = (x + 1) % NX, (x + NX - 1) % NX
    across = (x + 2) % NX
    share = NY * NZ // (NX * NC)

    def at(yy=None, zz=None, xx=None, cc=None):
        yy = y if yy is None else yy
        zz = z if zz is None else zz
        xx = x if xx is None else xx
        cc = c if cc is None else cc
        return (yy * NZ + zz, xx * NC + cc)

    labels = {}
    sent = []

    def slot(name):
        return labels.setdefault(name, len(labels))

    def send(name, source, target, device):
        k = slot(name)
        copy = pltpu.make_async_remote_copy(
            src_ref=source,
            dst_ref=target,
            send_sem=send_sems.at[k],
            recv_sem=recv_sems.at[k],
            device_id=device,
            device_id_type=MESH,
        )
        copy.start()
        sent.append(copy)
        return copy

    def receive(name, target):
        pltpu.make_async_copy(target, target, recv_sems.at[slot(name)]).wait()

    barrier = pltpu.get_barrier_semaphore()

    def greet(device):
        pl.semaphore_signal(barrier, inc=1, device_id=device, device_id_type=MESH)

    for d in range(1, NZ):
        greet(at(zz=(z + d) % NZ))
    for d in range(1, NY):
        greet(at(yy=(y + d) % NY))
    for d in range(1, NX * NC):
        other = (j + d) % (NX * NC)
        greet((i, other))
    count_ctx = NY * NZ
    greet(((i + 1) % count_ctx, j))
    greet(((i + count_ctx - 1) % count_ctx, j))
    swap_to = (share * j + i % share, i // share)
    swap_from = (share * j + i % share, i // share)
    moves = jnp.logical_or(swap_to[0] != i, swap_to[1] != j)

    @pl.when(moves)
    def _():
        greet(swap_to)

    partners = NZ - 1 + NY - 1 + NX * NC - 1 + 2
    pl.semaphore_wait(barrier, partners + jnp.where(moves, 1, 0))

    parts = (("kv", 256, 512), ("q", 0, 256))
    own_cols = pl.ds(aligned(y, 128), 128)
    for name, first, rows in parts[:1]:
        block = wt_ref.at[pl.ds(first, rows), :]
        target = wbuf.at[pl.ds(first, rows), own_cols]
        send("w_up_" + name, block, target, at(yy=up))
        send("w_down_" + name, block, target, at(yy=down))
    emb_piece = emb_ref.at[pl.ds(aligned(y, 128), 128), pl.ds(aligned(z % share, 128), 128)]
    holder = z // share
    e_slots = [slot("e" + str(k)) for k in range(NX)]
    e_sends = [slot("es" + str(k)) for k in range(NX * NC)]

    def emb_copies():
        copies = []
        for d in range(1, NX * NC):
            other = (j + d) % (NX * NC)
            copies.append(
                pltpu.make_async_remote_copy(
                    src_ref=emb_piece,
                    dst_ref=ebuf.at[x],
                    send_sem=send_sems.at[e_sends[d]],
                    recv_sem=recv_sems.at[e_slots[0] + x],
                    device_id=(i, other),
                    device_id_type=MESH,
                )
            )
        return copies

    @pl.when(c == holder)
    def _():
        for copy in emb_copies():
            copy.start()
        pltpu.make_async_copy(emb_piece, ebuf.at[x], recv_sems.at[e_slots[0] + x]).start()

    for name, first, rows in parts[1:]:
        block = wt_ref.at[pl.ds(first, rows), :]
        target = wbuf.at[pl.ds(first, rows), own_cols]
        send("w_up_" + name, block, target, at(yy=up))
        send("w_down_" + name, block, target, at(yy=down))
    send("tokens", tokens_ref.at[:, pl.ds(384, 128)], before, ((i + 1) % count_ctx, j))

    wo_rows = pl.ds(aligned(2 * y + z // share, 256), 256)
    wo_cols = pl.ds(aligned(z % share, 128), 128)
    swap_rows = pl.ds(aligned(j, 256), 256)
    swap_slot = slot("swap")

    def swap_copy():
        return pltpu.make_async_remote_copy(
            src_ref=ow_ref,
            dst_ref=wo.at[swap_rows, wo_cols],
            send_sem=send_sems.at[swap_slot],
            recv_sem=recv_sems.at[swap_slot],
            device_id=swap_to,
            device_id_type=MESH,
        )

    @pl.when(moves)
    def _():
        swap_copy().start()

    @pl.when(jnp.logical_not(moves))
    def _():
        pltpu.make_async_copy(ow_ref, wo.at[wo_rows, wo_cols], recv_sems.at[swap_slot]).start()

    wbuf[:, own_cols] = wt_ref[...]

    lane = lax.broadcasted_iota(jnp.int32, (CHUNK, CHUNK), 1)
    row = lax.broadcasted_iota(jnp.int32, (CHUNK, CHUNK), 0)
    lane_f = lane.astype(f32)
    row_f = row.astype(f32)
    filters = jnp.zeros((GROUP, CHUNK), f32)
    grid = lax.broadcasted_iota(jnp.int32, (GROUP, CHUNK), 1).astype(f32)
    for m in range(16):
        rate = modes_ref[0, :, m : m + 1]
        filters = filters + modes_ref[1, :, m : m + 1] * jnp.exp(-rate * grid)
    for g in range(16):
        wide = jnp.broadcast_to(filters[g : g + 1, :], (CHUNK, CHUNK))
        rolled = pltpu.roll(wide, 0, 1, stride=1, stride_axis=0)
        high, low = split(jnp.where(lane >= row, rolled, 0.0))
        toep_high[g] = high
        toep_low[g] = low
    for h in range(2):
        to_end[h] = jnp.exp(-rate_row_ref[h : h + 1, :] * (CHUNK - 1 - row_f))
        rate_col = cols_ref[h * 128 : (h + 1) * 128, 1:2]
        res_col = cols_ref[h * 128 : (h + 1) * 128, 2:3]
        from_end[h] = res_col * jnp.exp(-rate_col * (lane_f + 1.0))

    def relay(tag, buffer, name, first, rows):
        half = rows // 2
        from_down = buffer.at[pl.ds(first, rows), pl.ds(aligned(down, 128), 128)]
        receive(tag + "_up_" + name, from_down)
        block = buffer.at[pl.ds(first, half), pl.ds(aligned(down, 128), 128)]
        send(tag + "_on_up_" + name, block, block, at(yy=up))
        from_up = buffer.at[pl.ds(first, rows), pl.ds(aligned(up, 128), 128)]
        receive(tag + "_down_" + name, from_up)
        block = buffer.at[pl.ds(first + half, half), pl.ds(aligned(up, 128), 128)]
        send(tag + "_on_down_" + name, block, block, at(yy=down))

    def relayed(tag, buffer, name, first, rows):
        half = rows // 2
        columns = pl.ds(aligned(opposite, 128), 128)
        receive(tag + "_on_up_" + name, buffer.at[pl.ds(first, half), columns])
        receive(tag + "_on_down_" + name, buffer.at[pl.ds(first + half, half), columns])

    relay("w", wbuf, *parts[0])

    for k in range(NX):
        pltpu.make_async_copy(ebuf.at[k], ebuf.at[k], recv_sems.at[e_slots[k]]).wait()
    ones = jnp.ones((8, 128), bf16)
    square_sum = jnp.zeros((8, 128), f32)
    for k in range(NX):
        piece = ebuf[k].astype(f32)
        high, low = split(piece * piece)
        square_sum = square_sum + dot_nt(ones, high) + dot_nt(ones, low)
        gain = gain_ref[pl.ds(k * NZ + z, 1), :]
        enorm[:, k * 128 : (k + 1) * 128] = (piece * gain).astype(bf16)
    squares[z] = square_sum
    for d in range(1, NZ):
        send("sq" + str(d), squares.at[z], squares.at[z], at(zz=(z + d) % NZ))

    def table_part(name, first, rows):
        piece = rows // NZ
        value = dot_nt(wbuf[first : first + rows, :], enorm[...])
        partial[first : first + rows, :] = value
        partial16[first : first + rows, :] = value.astype(bf16)
        for d in range(1, NZ):
            to = (z + d) % NZ
            source = partial16.at[pl.ds(first + aligned(to, piece), piece), :]
            target = arrived.at[z, pl.ds(first // NZ, piece), :]
            send("rs_" + name + str(d), source, target, at(zz=to))

    relayed("w", wbuf, *parts[0])
    table_part(*parts[0])
    relay("w", wbuf, *parts[1])

    receive("tokens", before)
    earlier = jnp.where(i > 0, before[...], -1)
    vocab_row = lax.broadcasted_iota(jnp.int32, (512, 128), 0)
    one_hot[:, 0:128] = jnp.where(vocab_row == earlier, 1.0, 0.0).astype(bf16)
    for k in range(4):
        these = tokens_ref[:, k * 128 : (k + 1) * 128]
        one_hot[:, (k + 1) * 128 : (k + 2) * 128] = jnp.where(vocab_row == these, 1.0, 0.0).astype(bf16)

    relayed("w", wbuf, *parts[1])
    table_part(*parts[1])

    for d in range(1, NZ):
        receive("sq" + str(d), squares.at[(z + NZ - d) % NZ])
    all_squares = squares[0]
    for k in range(1, NZ):
        all_squares = all_squares + squares[k]
    width = gain_ref.shape[0] * gain_ref.shape[1]
    scale = lax.rsqrt(all_squares * (1.0 / width) + 1e-05)[0:1, :]

    def reduce_part(name, first, rows):
        piece = rows // NZ
        mine = pl.ds(first + aligned(z, piece), piece)
        value = partial[mine, :]
        for d in range(1, NZ):
            origin = (z + NZ - d) % NZ
            receive("rs_" + name + str(d), arrived.at[origin, pl.ds(first // NZ, piece), :])
            value = value + arrived[origin, first // NZ : first // NZ + piece, :].astype(f32)
        table[mine, own_cols] = (value * scale).astype(bf16)
        block = table.at[mine, own_cols]
        for d in range(1, NZ):
            send("ag_" + name + str(d), block, block, at(zz=(z + d) % NZ))

    def spread_part(name, first, rows):
        piece = rows // NZ
        for d in range(1, NZ):
            origin = (z + NZ - d) % NZ
            receive("ag_" + name + str(d), table.at[pl.ds(first + aligned(origin, piece), piece), own_cols])
        block = table.at[pl.ds(first, rows), own_cols]
        send("t_up_" + name, block, block, at(yy=up))
        send("t_down_" + name, block, block, at(yy=down))

    reduce_part(*parts[0])
    reduce_part(*parts[1])
    spread_part(*parts[0])
    spread_part(*parts[1])

    pltpu.make_async_copy(wo.at[wo_rows, wo_cols], wo.at[wo_rows, wo_cols], recv_sems.at[swap_slot]).wait()
    for d in range(1, NZ):
        block = wo.at[wo_rows, wo_cols]
        send("wz" + str(d), block, block, at(zz=(z + d) % NZ))

    relay("t", table, *parts[0])
    relay("t", table, *parts[1])
    relayed("t", table, *parts[0])

    def short_conv(base, g, part):
        value = proj[pl.ds(base + aligned(g, 16), 16), :]
        taps = cols_ref[pl.ds(aligned(g, 16), 16), :]
        result = taps[:, 3 + 7 * part : 4 + 7 * part] * value[:, 128:]
        for lag in range(1, 7):
            k = 3 + 7 * part + lag
            result = result + taps[:, k : k + 1] * pltpu.roll(value, lag, 1)[:, 128:]
        return result

    proj[256:768, :] = dot(table[256:768, :], one_hot[...])

    def drive(g, carry):
        value = short_conv(256, g, 1) * short_conv(512, g, 2)
        for k in range(4):
            driving[g, k] = value[:, k * 128 : (k + 1) * 128]
        return carry

    lax.fori_loop(0, 16, drive, 0)

    own_lanes = lax.broadcasted_iota(jnp.int32, (8, 64, 128), 2) // 16 == lax.broadcasted_iota(
        jnp.int32, (8, 64, 128), 0
    )
    for h in range(2):
        blocks = driving[h * 8 : (h + 1) * 8].reshape(512, 128)
        value = dot_three(blocks, to_end[h]).reshape(8, 64, 128)
        value = jnp.sum(jnp.where(own_lanes, value, 0.0), axis=0)
        ends[h] = value.reshape(4, 16, 128)
        over = jnp.exp(-float(CHUNK) * rate_row_ref[h : h + 1, :])
        state = ends[h, 0]
        for k in range(1, 4):
            state = over * state + ends[h, k]
        zstate[z, h * 16 : (h + 1) * 16, :] = state
    for d in range(1, NZ):
        send("sz" + str(d), zstate.at[z], zstate.at[z], at(zz=(z + d) % NZ))

    relayed("t", table, *parts[1])
    proj[0:256, :] = dot(table[0:256, :], one_hot[...])

    def ask(g, carry):
        queries[pl.ds(aligned(g, 16), 16), :] = short_conv(0, g, 0)
        return carry

    lax.fori_loop(0, 16, ask, 0)

    def inside(g, carry):
        high, low = split(driving[g].reshape(64, 128))
        conv[g] = dot(high, toep_high[g]) + dot(low, toep_high[g]) + dot(high, toep_low[g])
        return carry

    lax.fori_loop(0, 16, inside, 0)

    block_rate = -512.0

    def power(h, steps):
        weight = jnp.exp(rate_row_ref[h : h + 1, :] * (block_rate * jnp.maximum(steps, 0).astype(f32)))
        return jnp.where(steps >= 0, weight, 0.0)

    for d in range(1, NZ):
        receive("sz" + str(d), zstate.at[(z + NZ - d) % NZ])
    for h in range(2):
        part = slice(h * 16, (h + 1) * 16)
        line = jnp.zeros((16, 128), f32)
        for k in range(NZ):
            line = line + power(h, jnp.int32(NZ - 1 - k)) * zstate[k, part, :]
        ystate[y, part, :] = line
    for d in range(1, NY):
        send("sy" + str(d), ystate.at[y], ystate.at[y], at(yy=(y + d) % NY))

    for d in range(1, NZ):
        origin = (z + NZ - d) % NZ
        receive(
            "wz" + str(d),
            wo.at[
                pl.ds(aligned(2 * y + origin // share, 256), 256),
                pl.ds(aligned(origin % share, 128), 128),
            ],
        )
    wo_line = wo.at[pl.ds(aligned(y, 512), 512), :]
    send("wy_up", wo_line, wo_line, at(yy=up))
    send("wy_down", wo_line, wo_line, at(yy=down))

    starts = []
    for h in range(2):
        part = slice(h * 16, (h + 1) * 16)
        start = jnp.zeros((16, 128), f32)
        for k in range(NZ):
            start = start + power(h, z - 1 - k) * zstate[k, part, :]
        starts.append(start)
    for d in range(1, NY):
        receive("sy" + str(d), ystate.at[(y + NY - d) % NY])
    for h in range(2):
        part = slice(h * 16, (h + 1) * 16)
        start = starts[h]
        for k in range(NY):
            steps = jnp.where(k < y, z + NZ * (y - 1 - k), -1)
            start = start + power(h, steps) * ystate[k, part, :]
        over = jnp.exp(-float(CHUNK) * rate_row_ref[h : h + 1, :])
        states = [start]
        for k in range(3):
            states.append(over * states[-1] + ends[h, k])
        state = jnp.concatenate(states, axis=0)
        wide = jnp.where(own_lanes, jnp.broadcast_to(state[None], (8, 64, 128)), 0.0)
        value = dot_three(wide.reshape(512, 128), from_end[h]).reshape(8, 64, 128)
        conv[h * 8 : (h + 1) * 8] = conv[h * 8 : (h + 1) * 8] + value

    def gate(g, carry):
        here = pl.ds(aligned(g, 16), 16)
        skip = cols_ref[here, 0:1]
        for k in range(4):
            response = conv[g, k * 16 : (k + 1) * 16, :] + skip * driving[g, k]
            gated_t[here, k * 128 : (k + 1) * 128] = queries[here, k * 128 : (k + 1) * 128] * response
        return carry

    lax.fori_loop(0, 16, gate, 0)
    for k in range(4):
        for h in range(2):
            block = gated_t[h * 128 : (h + 1) * 128, k * 128 : (k + 1) * 128]
            gated[j, k * 128 : (k + 1) * 128, h * 128 : (h + 1) * 128] = block.T.astype(bf16)

    halves = (pl.ds(0, 256), pl.ds(256, 256))
    own = [gated.at[j, half, :] for half in halves]
    send("g_right0", own[0], own[0], at(xx=right))
    send("g_left1", own[1], own[1], at(xx=left))
    send("g_right1", own[1], own[1], at(xx=right))
    send("g_left0", own[0], own[0], at(xx=left))
    send("g_mate", gated.at[j], gated.at[j], at(cc=1 - c))

    wo_down = pl.ds(aligned(down, 512), 512)
    wo_up = pl.ds(aligned(up, 512), 512)
    receive("wy_up", wo.at[wo_down, :])
    block = wo.at[pl.ds(aligned(2 * down, 256), 256), :]
    send("wy_on_up", block, block, at(yy=up))
    receive("wy_down", wo.at[wo_up, :])
    block = wo.at[pl.ds(aligned(2 * up + 1, 256), 256), :]
    send("wy_on_down", block, block, at(yy=down))

    left_j, right_j, across_j = left * NC + c, right * NC + c, across * NC + c
    from_left = [gated.at[left_j, half, :] for half in halves]
    from_right = [gated.at[right_j, half, :] for half in halves]
    from_across = [gated.at[across_j, half, :] for half in halves]
    mate = at(cc=1 - c)
    receive("g_right0", from_left[0])
    send("g_on_right", from_left[0], from_left[0], at(xx=right))
    receive("g_left1", from_right[1])
    send("g_on_left", from_right[1], from_right[1], at(xx=left))
    send("m_left0", from_left[0], from_left[0], mate)
    send("m_right1", from_right[1], from_right[1], mate)
    receive("g_right1", from_left[1])
    send("m_left1", from_left[1], from_left[1], mate)
    receive("g_left0", from_right[0])
    send("m_right0", from_right[0], from_right[0], mate)

    receive("wy_on_up", wo.at[pl.ds(aligned(2 * opposite, 256), 256), :])
    receive("wy_on_down", wo.at[pl.ds(aligned(2 * opposite + 1, 256), 256), :])

    def product(index):
        return dot(gated[index], wo[pl.ds(aligned(index, 256), 256), :])

    mate_j = x * NC + 1 - c
    total[...] = product(j)
    receive("g_mate", gated.at[mate_j])
    total[...] += product(mate_j)
    total[...] += product(left_j)
    total[...] += product(right_j)
    receive("g_on_right", from_across[0])
    send("m_across0", from_across[0], from_across[0], mate)
    receive("g_on_left", from_across[1])
    send("m_across1", from_across[1], from_across[1], mate)
    for name, place in (("left", left), ("right", right), ("across", across)):
        index = place * NC + 1 - c
        if name == "across":
            total[...] += product(across_j)
        receive("m_" + name + "0", gated.at[index, halves[0], :])
        receive("m_" + name + "1", gated.at[index, halves[1], :])
        if name == "across":
            out_ref[...] = (total[...] + product(index)).astype(bf16)
        else:
            total[...] += product(index)

    for copy in sent:
        copy.wait_send()

    @pl.when(c == holder)
    def _():
        for copy in emb_copies():
            copy.wait_send()

    @pl.when(moves)
    def _():
        swap_copy().wait_send()


SEMAPHORES = 112


def body(
    tokens,
    embedding,
    norm_gain,
    in_weight,
    short_taps,
    decay_rates,
    residue,
    skip_weight,
    out_weight,
):
    rates = decay_rates.T
    residues = residue.T
    cols = jnp.concatenate(
        [
            skip_weight[:, None],
            rates.reshape(256, 1),
            residues.reshape(256, 1),
            short_taps.transpose(2, 1, 0).reshape(256, 21),
        ],
        axis=1,
    )
    wt = in_weight.transpose(1, 2, 0).reshape(768, 128)
    whole = pl.BlockSpec(memory_space=pltpu.VMEM)
    outside = pl.BlockSpec(memory_space=pl.ANY)
    vm = pltpu.VMEM
    return pl.pallas_call(
        kernel,
        out_shape=jax.ShapeDtypeStruct((512, 512), bf16),
        in_specs=[whole] * 6 + [outside] * 2,
        out_specs=whole,
        scratch_shapes=[
            vm((1, 128), jnp.int32),
            vm((NX, 128, 128), bf16),
            vm((128, 512), bf16),
            vm((768, 512), bf16),
            vm((NZ, 8, 128), f32),
            vm((768, 128), f32),
            vm((768, 128), bf16),
            vm((NZ, 96, 128), bf16),
            vm((768, 512), bf16),
            vm((512, 640), bf16),
            vm((768, 640), f32),
            vm((16, 4, 16, 128), f32),
            vm((16, 64, 128), f32),
            vm((256, 512), f32),
            vm((16, 128, 128), bf16),
            vm((16, 128, 128), bf16),
            vm((2, 128, 128), f32),
            vm((2, 128, 128), f32),
            vm((NZ, 32, 128), f32),
            vm((NY, 32, 128), f32),
            vm((2, 4, 16, 128), f32),
            vm((256, 512), f32),
            vm((NX * NC, 512, 256), bf16),
            vm((2048, 512), bf16),
            vm((512, 512), f32),
            pltpu.SemaphoreType.DMA((SEMAPHORES,)),
            pltpu.SemaphoreType.DMA((SEMAPHORES,)),
        ],
        compiler_params=pltpu.CompilerParams(
            collective_id=0, has_side_effects=True, vmem_limit_bytes=48 * 1024 * 1024
        ),
    )(
        tokens.reshape(1, 512),
        norm_gain.reshape(32, 128),
        cols,
        rates.reshape(2, 128),
        jnp.stack([rates, residues]),
        wt,
        embedding,
        out_weight,
    )


def solution(mesh):
    placed = (
        P("ctx"),
        P(None, "fsdp"),
        P(),
        P("ctx", None, "fsdp"),
        P(None, None, "fsdp"),
        P(None, "fsdp"),
        P(None, "fsdp"),
        P("fsdp"),
        P("fsdp", "ctx"),
    )
    return jax.shard_map(
        body, mesh=mesh, in_specs=placed, out_specs=P("ctx", "fsdp"), check_vma=False
    )
```

```python
import functools

import jax
import jax.numpy as jnp
from jax import lax
from jax.experimental import pallas as pl
from jax.experimental.pallas import tpu as pltpu
from jax.sharding import PartitionSpec as P

GROUP = 16
CHUNK = 128
NY, NZ, NX, NC = 4, 8, 4, 2
f32 = jnp.float32
bf16 = jnp.bfloat16
MESH = pl.DeviceIdType.MESH


def split(value):
    high = value.astype(bf16)
    return high, (value - high.astype(f32)).astype(bf16)


def dot(a, b):
    return jnp.dot(a, b, preferred_element_type=f32)


def dot_three(a, b):
    a_high, a_low = split(a)
    b_high, b_low = split(b)
    return dot(a_high, b_high) + dot(a_low, b_high) + dot(a_high, b_low)


def dot_nt(a, b):
    return lax.dot_general(a, b, (((1,), (1,)), ((), ())), preferred_element_type=f32)


def aligned(index, size):
    return pl.multiple_of(index * size, size)


def kernel(
    tokens_ref,
    gain_ref,
    skip_ref,
    taps_ref,
    rates_ref,
    residue_ref,
    w_ref,
    emb_ref,
    ow_ref,
    out_ref,
    wt,
    wbuf,
    ebuf,
    enorm,
    squares,
    send_kv,
    send_q,
    arrived_kv,
    arrived_q,
    own_kv,
    own_q,
    table,
    tokens,
    token_mat,
    one_hot,
    short_in,
    taps,
    driving,
    queries,
    convolved,
    gated_f,
    gated_b,
    landed,
    gated,
    wo,
    total,
    send_sems,
    recv_sems,
):
    i = lax.axis_index("ctx")
    j = lax.axis_index("fsdp")
    y, z = i // NZ, i % NZ
    x, c = j // NC, j % NC
    up, down = (y + 1) % NY, (y + NY - 1) % NY
    opposite = (y + 2) % NY
    right, left = (x + 1) % NX, (x + NX - 1) % NX
    across = (x + 2) % NX
    count_ctx = NY * NZ
    count_fsdp = NX * NC
    share = count_ctx // count_fsdp

    def at(yy=None, zz=None, xx=None, cc=None):
        yy = y if yy is None else yy
        zz = z if zz is None else zz
        xx = x if xx is None else xx
        cc = c if cc is None else cc
        return (yy * NZ + zz, xx * NC + cc)

    labels = {}
    sent = []

    def slot(name):
        return labels.setdefault(name, len(labels))

    def remote(name, source, target, device):
        k = slot(name)
        return pltpu.make_async_remote_copy(
            src_ref=source,
            dst_ref=target,
            send_sem=send_sems.at[k],
            recv_sem=recv_sems.at[k],
            device_id=device,
            device_id_type=MESH,
        )

    def send(name, source, target, device):
        copy = remote(name, source, target, device)
        copy.start()
        sent.append(copy)

    def receive(name, target):
        pltpu.make_async_copy(target, target, recv_sems.at[slot(name)]).wait()

    barrier = pltpu.get_barrier_semaphore()

    def greet(device):
        pl.semaphore_signal(barrier, inc=1, device_id=device, device_id_type=MESH)

    for d in range(1, count_ctx):
        greet(((i + d) % count_ctx, j))
    for d in range(1, count_fsdp):
        greet((i, (j + d) % count_fsdp))
    swap_to = (share * j + i % share, i // share)
    moves = jnp.logical_or(swap_to[0] != i, swap_to[1] != j)

    @pl.when(moves)
    def _():
        greet(swap_to)

    for group in range(3):
        for h in range(2):
            block = w_ref[group, :, h * 128 : (h + 1) * 128].astype(f32)
            wt[group, h * 128 : (h + 1) * 128, :] = block.T.astype(bf16)
    ones = jnp.ones((8, 512), bf16)
    piece = emb_ref[...].astype(f32)
    high, low = split(piece * piece)
    squares[j] = (dot_nt(ones, high) + dot_nt(ones, low))[0:1, :]

    pl.semaphore_wait(barrier, count_ctx - 1 + count_fsdp - 1 + jnp.where(moves, 1, 0))

    holder = z // share
    e_slots = [slot("e" + str(k)) for k in range(NX)]
    emb_piece = emb_ref.at[:, pl.ds(aligned(z % share, 128), 128)]

    def emb_copy(k, source, place, device):
        return pltpu.make_async_remote_copy(
            src_ref=source,
            dst_ref=ebuf.at[place],
            send_sem=send_sems.at[slot("es" + str(k))],
            recv_sem=recv_sems.at[e_slots[0] + place],
            device_id=device,
            device_id_type=MESH,
        )

    mate = at(cc=1 - c)

    def emb_copies():
        copies = [emb_copy(d, emb_piece, x, at(xx=(x + d) % NX)) for d in (2, 1, 3)]
        return copies + [emb_copy(0, emb_piece, x, mate)]

    def emb_relays():
        places = [(x + d) % NX for d in (1, 3, 2)]
        return [(place, emb_copy(4 + n, ebuf.at[place], place, mate)) for n, place in enumerate(places)]

    @pl.when(c == holder)
    def _():
        for copy in emb_copies():
            copy.start()
        pltpu.make_async_copy(emb_piece, ebuf.at[x], recv_sems.at[e_slots[0] + x]).start()

    def w_rows(to):
        return wt.at[:, pl.ds(aligned(to, 64), 64), :]

    for d in (2, 1, 3):
        to = (y + d) % NY
        send("w" + str(d), w_rows(to), wbuf.at[y], at(yy=to))

    for d in range(1, NZ):
        send("tz" + str(d), tokens_ref, tokens.at[y, z], at(zz=(z + d) % NZ))
    for d in range(1, count_fsdp):
        send("sq" + str(d), squares.at[j], squares.at[j], (i, (j + d) % count_fsdp))

    wo_rows = pl.ds(aligned(2 * y + z // share, 256), 256)
    wo_cols = pl.ds(aligned(z % share, 128), 128)
    wo_own = wo.at[wo_rows, wo_cols]

    def swap_copy():
        return remote("swap", ow_ref, wo.at[pl.ds(aligned(j, 256), 256), wo_cols], swap_to)

    @pl.when(moves)
    def _():
        swap_copy().start()

    @pl.when(jnp.logical_not(moves))
    def _():
        pltpu.make_async_copy(ow_ref, wo_own, recv_sems.at[slot("swap")]).start()

    wbuf[y] = wt[:, pl.ds(aligned(y, 64), 64), :]
    tokens[y, z] = tokens_ref[...]

    row = lax.broadcasted_iota(jnp.int32, (CHUNK, CHUNK), 0)
    lane = lax.broadcasted_iota(jnp.int32, (CHUNK, CHUNK), 1)
    group_lane = lax.broadcasted_iota(jnp.int32, (16, 16), 1) == i // 2
    rate = jnp.sum(jnp.where(group_lane, rates_ref[...], 0.0), axis=1, keepdims=True)
    weight = jnp.sum(jnp.where(group_lane, residue_ref[...], 0.0), axis=1, keepdims=True)
    steps = lax.broadcasted_iota(jnp.int32, (16, CHUNK), 1).astype(f32)
    rate = jnp.broadcast_to(rate, (16, CHUNK))
    weight = jnp.broadcast_to(weight, (16, CHUNK))
    filters = jnp.sum(weight * jnp.exp(-rate * steps), axis=0, keepdims=True)
    rolled = pltpu.roll(jnp.broadcast_to(filters, (CHUNK, CHUNK)), 0, 1, stride=1, stride_axis=0)
    toeplitz = jnp.where(lane >= row, rolled, 0.0).T
    to_end = jnp.exp(-rate * (CHUNK - 1 - steps))
    from_start = weight * jnp.exp(-rate * (steps + 1.0))
    from_start = jnp.concatenate([from_start, jnp.zeros((CHUNK - 16, CHUNK), f32)], axis=0).T

    pick = lax.broadcasted_iota(jnp.int32, (8, 256), 1) == 8 * i + lax.broadcasted_iota(jnp.int32, (8, 256), 0)
    skips = jnp.sum(jnp.where(pick, skip_ref[...], 0.0), axis=1, keepdims=True)
    skips = jnp.broadcast_to(skips, (8, CHUNK))
    for group in range(3):
        for lag in range(7):
            value = jnp.where(pick, taps_ref[group, lag : lag + 1, :], 0.0)
            taps[group, lag] = jnp.broadcast_to(jnp.sum(value, axis=1, keepdims=True), (8, CHUNK))

    @pl.when(c == holder)
    def _():
        pltpu.make_async_copy(ebuf.at[x], ebuf.at[x], recv_sems.at[e_slots[0] + x]).wait()
        for place, copy in emb_relays():
            pltpu.make_async_copy(ebuf.at[place], ebuf.at[place], recv_sems.at[e_slots[0] + place]).wait()
            copy.start()

    @pl.when(c != holder)
    def _():
        for k in range(NX):
            pltpu.make_async_copy(ebuf.at[k], ebuf.at[k], recv_sems.at[e_slots[k]]).wait()

    for k in range(NY):
        gain = gain_ref[pl.ds(k * NZ + z, 1), :]
        enorm[:, k * 128 : (k + 1) * 128] = (ebuf[k].astype(f32) * gain).astype(bf16)
    for d in range(1, NY):
        receive("w" + str(d), wbuf.at[(y + NY - d) % NY])

    def partial(group):
        weights = jnp.concatenate([wbuf[k, group] for k in range(NY)], axis=1)
        return dot_nt(weights, enorm[...])

    keys, values = partial(1), partial(2)
    for k in range(NZ):
        part = slice(k * 8, (k + 1) * 8)
        send_kv[k] = jnp.concatenate([keys[part], values[part]], axis=0).astype(bf16)
    for d in (4, 3, 5, 2, 6, 1, 7):
        to = (z + d) % NZ
        send("kv" + str(d), send_kv.at[to], arrived_kv.at[z], at(zz=to))
    asks = partial(0)
    for k in range(NZ):
        part = slice(k * 8, (k + 1) * 8)
        send_q[k] = jnp.concatenate([asks[part, 0:256], asks[part, 256:512]], axis=0).astype(bf16)
    for d in (4, 3, 5, 2, 6, 1, 7):
        to = (z + d) % NZ
        send("q" + str(d), send_q.at[to], arrived_q.at[z], at(zz=to))
    own_kv[...] = send_kv[z].astype(f32)
    own_q[...] = send_q[z].astype(f32)

    for d in range(1, NZ):
        receive("tz" + str(d), tokens.at[y, (z + NZ - d) % NZ])
    for d in range(1, NY):
        send("ty" + str(d), tokens.at[y], tokens.at[y], at(yy=(y + d) % NY))

    receive("swap", wo_own)
    for d in (2, 6, 1, 7):
        send("wz" + str(d), wo_own, wo_own, at(zz=(z + d) % NZ))

    for d in range(1, NY):
        receive("ty" + str(d), tokens.at[(y + NY - d) % NY])
    for k in range(count_ctx):
        token_mat[k * 4 : (k + 1) * 4, :] = tokens[k // NZ, k % NZ].astype(f32)
    token_mat[...] = token_mat[...].T
    vocab_row = lax.broadcasted_iota(jnp.int32, (512, 128), 0).astype(f32)

    def mark(n, carry):
        for h in range(2):
            these = token_mat[pl.ds(2 * n + h, 1), :]
            hits = jnp.where(vocab_row == these, 1.0, 0.0)
            one_hot[n, :, h * 128 : (h + 1) * 128] = hits.astype(bf16)
        return carry

    lax.fori_loop(0, 64, mark, 0)

    def wo_place(origin, half=None):
        rows, first = (256, 0) if half is None else (128, half * 128)
        return wo.at[
            pl.ds(aligned(2 * y + origin // share, 256) + first, rows),
            pl.ds(aligned(origin % share, 128), 128),
        ]

    for d in range(1, count_fsdp):
        receive("sq" + str(d), squares.at[(j + count_fsdp - d) % count_fsdp])
    all_squares = squares[0]
    for k in range(1, count_fsdp):
        all_squares = all_squares + squares[k]
    width = gain_ref.shape[0] * gain_ref.shape[1]
    scale = lax.rsqrt(all_squares * (1.0 / width) + 1e-05)

    value = own_kv[...]
    for d in (1, 7, 2, 6, 3, 5, 4):
        origin = (z + NZ - d) % NZ
        receive("kv" + str(d), arrived_kv.at[origin])
        value = value + arrived_kv[origin].astype(f32)
    table[8:24, :] = value * scale
    value = own_q[...]
    for d in (1, 7, 2, 6, 3, 5, 4):
        origin = (z + NZ - d) % NZ
        receive("q" + str(d), arrived_q.at[origin])
        value = value + arrived_q[origin].astype(f32)
    table[0:8, :] = jnp.concatenate([value[0:8], value[8:16]], axis=1) * scale
    table[24:32, :] = jnp.zeros((8, 512), f32)

    for d in (1, 7, 2, 6):
        receive("wz" + str(d), wo_place((z + NZ - d) % NZ))
    ahead, behind = at(zz=(z + 2) % NZ), at(zz=(z + NZ - 2) % NZ)
    block = wo_place((z + NZ - 1) % NZ)
    send("wz3", block, block, ahead)
    block = wo_place((z + 1) % NZ)
    send("wz5", block, block, behind)
    block = wo_place((z + NZ - 2) % NZ, 0)
    send("wz4a", block, block, ahead)
    block = wo_place((z + 2) % NZ, 1)
    send("wz4b", block, block, behind)

    table16 = table[...].astype(bf16)

    def look_up(n, carry):
        found = dot(table16, one_hot[n])
        for group in range(3):
            for h in range(2):
                rows = pl.ds(aligned(2 * n + h + 8, 8), 8)
                short_in[group, rows, :] = found[group * 8 : (group + 1) * 8, h * 128 : (h + 1) * 128]
        return carry

    lax.fori_loop(0, 64, look_up, 0, unroll=4)
    for group in range(3):
        tail = short_in[group, 1024:1088, :]
        shifted = pltpu.roll(tail, 1, 1)
        first_lane = lax.broadcasted_iota(jnp.int32, (64, 128), 1) == 0
        short_in[group, 0:64, :] = jnp.where(first_lane, 0.0, shifted)

    def convolve(n, carry):
        sums = []
        for group in range(3):
            result = taps[group, 0] * short_in[group, pl.ds(aligned(n + 8, 8), 8), :]
            for lag in range(1, 7):
                rows = pl.ds(aligned(n + 8 - lag, 8), 8)
                result = result + taps[group, lag] * short_in[group, rows, :]
            sums.append(result)
        here = pl.ds(aligned(n, 8), 8)
        queries[here, :] = sums[0]
        driving[here, :] = sums[1] * sums[2]
        return carry

    lax.fori_loop(0, 128, convolve, 0, unroll=4)

    receive("wz3", wo_place((z + NZ - 3) % NZ))
    receive("wz5", wo_place((z + 3) % NZ))
    receive("wz4a", wo_place((z + 4) % NZ, 0))
    receive("wz4b", wo_place((z + 4) % NZ, 1))
    wo_line = wo.at[pl.ds(aligned(y, 512), 512), :]
    send("wy_up", wo_line, wo_line, at(yy=up))
    send("wy_down", wo_line, wo_line, at(yy=down))

    planes = [driving[pl.ds(k, CHUNK, stride=8), :] for k in range(8)]
    wide = jnp.concatenate(planes, axis=1)
    ends = dot_three(to_end, wide)
    states = jnp.concatenate([ends[:, k * 128 : (k + 1) * 128] for k in range(8)], axis=0)
    rates = jnp.concatenate([rate] * 8, axis=0)

    def later(value, count):
        return jnp.where(lane >= count, pltpu.roll(value, count, 1), 0.0)

    for level in range(7):
        reach = 1 << level
        states = states + jnp.exp(-rates * float(CHUNK * reach)) * later(states, reach)
    states = later(states, 1)
    starts = jnp.concatenate([states[k * 16 : (k + 1) * 16] for k in range(8)], axis=1)
    starts = jnp.concatenate([starts, jnp.zeros((CHUNK - 16, 1024), f32)], axis=0)
    convolved[...] = dot_three(toeplitz, wide) + dot_three(from_start, starts)
    for k in range(8):
        response = convolved[:, k * 128 : (k + 1) * 128] + skips[k : k + 1, :] * planes[k]
        result = queries[pl.ds(k, CHUNK, stride=8), :] * response
        gated_f[pl.ds(k, CHUNK, stride=8), :] = result.T
    gated_b[...] = gated_f[...].astype(bf16)

    def positions(index):
        return gated_b.at[pl.ds(aligned(index, 32), 32), :]

    far = sorted(range(1, count_ctx), key=lambda d: -min(d % NZ, NZ - d % NZ))
    for d in far:
        to = (i + d) % count_ctx
        send("a" + str(d), positions(to), landed.at[i], (to, j))
    landed[i] = gated_b[pl.ds(aligned(i, 32), 32), :]
    for d in reversed(far):
        receive("a" + str(d), landed.at[(i + count_ctx - d) % count_ctx])
    for k in range(4):
        for h in range(2):
            blocks = [landed[n].astype(f32)[k * 8 : (k + 1) * 8] for n in range(h * 16, (h + 1) * 16)]
            block = jnp.concatenate(blocks, axis=0)
            gated[j, k * 128 : (k + 1) * 128, h * 128 : (h + 1) * 128] = block.T.astype(bf16)

    halves = (pl.ds(0, 256), pl.ds(256, 256))
    own = [gated.at[j, half, :] for half in halves]
    send("g_right0", own[0], own[0], at(xx=right))
    send("g_left1", own[1], own[1], at(xx=left))
    send("g_right1", own[1], own[1], at(xx=right))
    send("g_left0", own[0], own[0], at(xx=left))
    send("g_mate", gated.at[j], gated.at[j], at(cc=1 - c))

    wo_down = pl.ds(aligned(down, 512), 512)
    wo_up = pl.ds(aligned(up, 512), 512)
    receive("wy_up", wo.at[wo_down, :])
    block = wo.at[pl.ds(aligned(2 * down, 256), 256), :]
    send("wy_on_up", block, block, at(yy=up))
    receive("wy_down", wo.at[wo_up, :])
    block = wo.at[pl.ds(aligned(2 * up + 1, 256), 256), :]
    send("wy_on_down", block, block, at(yy=down))

    left_j, right_j, across_j = left * NC + c, right * NC + c, across * NC + c
    from_left = [gated.at[left_j, half, :] for half in halves]
    from_right = [gated.at[right_j, half, :] for half in halves]
    from_across = [gated.at[across_j, half, :] for half in halves]
    receive("g_right0", from_left[0])
    send("g_on_right", from_left[0], from_left[0], at(xx=right))
    receive("g_left1", from_right[1])
    send("g_on_left", from_right[1], from_right[1], at(xx=left))
    send("m_left0", from_left[0], from_left[0], mate)
    send("m_right1", from_right[1], from_right[1], mate)
    receive("g_right1", from_left[1])
    send("m_left1", from_left[1], from_left[1], mate)
    receive("g_left0", from_right[0])
    send("m_right0", from_right[0], from_right[0], mate)

    receive("wy_on_up", wo.at[pl.ds(aligned(2 * opposite, 256), 256), :])
    receive("wy_on_down", wo.at[pl.ds(aligned(2 * opposite + 1, 256), 256), :])

    def product(index):
        return dot(gated[index], wo[pl.ds(aligned(index, 256), 256), :])

    mate_j = x * NC + 1 - c
    total[...] = product(j)
    receive("g_mate", gated.at[mate_j])
    total[...] += product(mate_j)
    total[...] += product(left_j)
    total[...] += product(right_j)
    receive("g_on_right", from_across[0])
    send("m_across0", from_across[0], from_across[0], mate)
    receive("g_on_left", from_across[1])
    send("m_across1", from_across[1], from_across[1], mate)
    for name, place in (("left", left), ("right", right), ("across", across)):
        index = place * NC + 1 - c
        if name == "across":
            total[...] += product(across_j)
        receive("m_" + name + "0", gated.at[index, halves[0], :])
        receive("m_" + name + "1", gated.at[index, halves[1], :])
        if name == "across":
            out_ref[...] = (total[...] + product(index)).astype(bf16)
        else:
            total[...] += product(index)

    for copy in sent:
        copy.wait_send()

    @pl.when(c == holder)
    def _():
        for copy in emb_copies():
            copy.wait_send()
        for _, copy in emb_relays():
            copy.wait_send()

    @pl.when(moves)
    def _():
        swap_copy().wait_send()


SEMAPHORES = 160


def body(
    tokens,
    embedding,
    norm_gain,
    in_weight,
    short_taps,
    decay_rates,
    residue,
    skip_weight,
    out_weight,
):
    whole = pl.BlockSpec(memory_space=pltpu.VMEM)
    outside = pl.BlockSpec(memory_space=pl.ANY)
    vm = pltpu.VMEM
    return pl.pallas_call(
        kernel,
        out_shape=jax.ShapeDtypeStruct((512, 512), bf16),
        in_specs=[whole] * 8 + [outside],
        out_specs=whole,
        scratch_shapes=[
            vm((3, 256, 128), bf16),
            vm((NY, 3, 64, 128), bf16),
            vm((NX, 512, 128), bf16),
            vm((512, 512), bf16),
            vm((NX * NC, 1, 512), f32),
            vm((NZ, 16, 512), bf16),
            vm((NZ, 16, 256), bf16),
            vm((NZ, 16, 512), bf16),
            vm((NZ, 16, 256), bf16),
            vm((16, 512), f32),
            vm((16, 256), f32),
            vm((32, 512), f32),
            vm((NY, NZ, 4, 128), jnp.int32),
            vm((128, 128), f32),
            vm((64, 512, 256), bf16),
            vm((3, 1088, 128), f32),
            vm((3, 7, 8, 128), f32),
            vm((1024, 128), f32),
            vm((1024, 128), f32),
            vm((128, 1024), f32),
            vm((1024, 128), f32),
            vm((1024, 128), bf16),
            vm((NY * NZ, 32, 128), bf16),
            vm((NX * NC, 512, 256), bf16),
            vm((2048, 512), bf16),
            vm((512, 512), f32),
            pltpu.SemaphoreType.DMA((SEMAPHORES,)),
            pltpu.SemaphoreType.DMA((SEMAPHORES,)),
        ],
        compiler_params=pltpu.CompilerParams(
            collective_id=0, has_side_effects=True, vmem_limit_bytes=48 * 1024 * 1024
        ),
    )(
        tokens.reshape(4, 128),
        norm_gain.reshape(32, 128),
        skip_weight.reshape(1, 256),
        short_taps.transpose(1, 0, 2),
        decay_rates,
        residue,
        in_weight.transpose(1, 0, 2),
        embedding,
        out_weight,
    )


def solution(mesh):
    placed = (
        P("ctx"),
        P(None, "fsdp"),
        P(),
        P("ctx", None, "fsdp"),
        P(None, None, "fsdp"),
        P(None, "fsdp"),
        P(None, "fsdp"),
        P("fsdp"),
        P("fsdp", "ctx"),
    )
    return jax.shard_map(
        body, mesh=mesh, in_specs=placed, out_specs=P("ctx", "fsdp"), check_vma=False
    )
```

```python
import functools

import jax
import jax.numpy as jnp
from jax import lax
from jax.experimental import pallas as pl
from jax.experimental.pallas import tpu as pltpu
from jax.sharding import PartitionSpec as P

GROUP = 16
CHUNK = 128
NY, NZ, NX, NC = 4, 8, 4, 2
f32 = jnp.float32
bf16 = jnp.bfloat16
MESH = pl.DeviceIdType.MESH


def split(value):
    high = value.astype(bf16)
    return high, (value - high.astype(f32)).astype(bf16)


def dot(a, b):
    return jnp.dot(a, b, preferred_element_type=f32)


def dot_three(a, b):
    a_high, a_low = split(a)
    b_high, b_low = split(b)
    return dot(a_high, b_high) + dot(a_low, b_high) + dot(a_high, b_low)


def dot_nt(a, b):
    return lax.dot_general(a, b, (((1,), (1,)), ((), ())), preferred_element_type=f32)


def aligned(index, size):
    return pl.multiple_of(index * size, size)


def kernel(
    tokens_in,
    gain_in,
    skip_in,
    taps_in,
    rates_in,
    residue_in,
    w_in,
    emb_in,
    ow_ref,
    out_ref,
    tokens_ref,
    gain_ref,
    skip_ref,
    taps_ref,
    rates_ref,
    residue_ref,
    w_ref,
    emb_ref,
    wt,
    wbuf,
    ebuf,
    enorm,
    squares,
    send_kv,
    send_q,
    arrived_kv,
    arrived_q,
    own_kv,
    own_q,
    table,
    tokens,
    token_mat,
    token_page,
    one_hot,
    short_in,
    taps,
    driving,
    queries,
    convolved,
    gated_f,
    gated_b,
    landed,
    gated,
    wo,
    total,
    load_sems,
    send_sems,
    recv_sems,
):
    i = lax.axis_index("ctx")
    j = lax.axis_index("fsdp")
    y, z = i // NZ, i % NZ
    x, c = j // NC, j % NC
    up, down = (y + 1) % NY, (y + NY - 1) % NY
    opposite = (y + 2) % NY
    right, left = (x + 1) % NX, (x + NX - 1) % NX
    across = (x + 2) % NX
    count_ctx = NY * NZ
    count_fsdp = NX * NC
    share = count_ctx // count_fsdp

    def at(yy=None, zz=None, xx=None, cc=None):
        yy = y if yy is None else yy
        zz = z if zz is None else zz
        xx = x if xx is None else xx
        cc = c if cc is None else cc
        return (yy * NZ + zz, xx * NC + cc)

    labels = {}
    sent = []

    def slot(name):
        return labels.setdefault(name, len(labels))

    def remote(name, source, target, device):
        k = slot(name)
        return pltpu.make_async_remote_copy(
            src_ref=source,
            dst_ref=target,
            send_sem=send_sems.at[k],
            recv_sem=recv_sems.at[k],
            device_id=device,
            device_id_type=MESH,
        )

    def send(name, source, target, device):
        copy = remote(name, source, target, device)
        copy.start()
        sent.append(copy)

    def receive(name, target):
        pltpu.make_async_copy(target, target, recv_sems.at[slot(name)]).wait()

    def load(k, source, target):
        copy = pltpu.make_async_copy(source, target, load_sems.at[k])
        copy.start()
        return copy

    emb_load = load(0, emb_in, emb_ref)
    w_load = load(1, w_in, w_ref)
    small_loads = [
        load(2, tokens_in, tokens_ref),
        load(3, gain_in, gain_ref),
        load(4, skip_in, skip_ref),
        load(5, taps_in, taps_ref),
        load(6, rates_in, rates_ref),
        load(7, residue_in, residue_ref),
    ]

    barrier = pltpu.get_barrier_semaphore()

    def greet(device):
        pl.semaphore_signal(barrier, inc=1, device_id=device, device_id_type=MESH)

    for d in range(1, count_ctx):
        greet(((i + d) % count_ctx, j))
    for d in range(1, count_fsdp):
        greet((i, (j + d) % count_fsdp))
    swap_to = (share * j + i % share, i // share)
    moves = jnp.logical_or(swap_to[0] != i, swap_to[1] != j)

    @pl.when(moves)
    def _():
        greet(swap_to)

    w_load.wait()
    for group in range(3):
        for h in range(2):
            block = w_ref[group, :, h * 128 : (h + 1) * 128].astype(f32)
            wt[group, h * 128 : (h + 1) * 128, :] = block.T.astype(bf16)
    for copy in small_loads:
        copy.wait()
    pl.semaphore_wait(barrier, count_ctx - 1 + count_fsdp - 1 + jnp.where(moves, 1, 0))

    emb_load.wait()
    holder = z // share
    e_slots = [slot("e" + str(k)) for k in range(NX)]
    emb_piece = emb_ref.at[:, pl.ds(aligned(z % share, 128), 128)]

    def emb_copy(k, source, place, device):
        return pltpu.make_async_remote_copy(
            src_ref=source,
            dst_ref=ebuf.at[place],
            send_sem=send_sems.at[slot("es" + str(k))],
            recv_sem=recv_sems.at[e_slots[0] + place],
            device_id=device,
            device_id_type=MESH,
        )

    mate = at(cc=1 - c)

    def emb_copies():
        copies = [emb_copy(d, emb_piece, x, at(xx=(x + d) % NX)) for d in (2, 1, 3)]
        return copies + [emb_copy(0, emb_piece, x, mate)]

    def emb_relays():
        places = [(x + d) % NX for d in (1, 3, 2)]
        return [(place, emb_copy(4 + n, ebuf.at[place], place, mate)) for n, place in enumerate(places)]

    @pl.when(c == holder)
    def _():
        for copy in emb_copies():
            copy.start()
        pltpu.make_async_copy(emb_piece, ebuf.at[x], recv_sems.at[e_slots[0] + x]).start()

    def w_rows(to):
        return wt.at[:, pl.ds(aligned(to, 64), 64), :]

    for d in (2, 1, 3):
        to = (y + d) % NY
        send("w" + str(d), w_rows(to), wbuf.at[y], at(yy=to))

    for d in range(1, NZ):
        send("tz" + str(d), tokens_ref, tokens.at[y, z], at(zz=(z + d) % NZ))
    wo_rows = pl.ds(aligned(2 * y + z // share, 256), 256)
    wo_cols = pl.ds(aligned(z % share, 128), 128)
    wo_own = wo.at[wo_rows, wo_cols]

    def swap_copy():
        return remote("swap", ow_ref, wo.at[pl.ds(aligned(j, 256), 256), wo_cols], swap_to)

    @pl.when(moves)
    def _():
        swap_copy().start()

    @pl.when(jnp.logical_not(moves))
    def _():
        pltpu.make_async_copy(ow_ref, wo_own, recv_sems.at[slot("swap")]).start()

    wbuf[y] = wt[:, pl.ds(aligned(y, 64), 64), :]
    tokens[y, z] = tokens_ref[...]

    ones = jnp.ones((8, 512), bf16)
    piece = emb_ref[...].astype(f32)
    high, low = split(piece * piece)
    squares[j] = (dot_nt(ones, high) + dot_nt(ones, low))[0:1, :]

    for d in range(1, count_fsdp):
        send("sq" + str(d), squares.at[j], squares.at[j], (i, (j + d) % count_fsdp))

    row = lax.broadcasted_iota(jnp.int32, (CHUNK, CHUNK), 0)
    lane = lax.broadcasted_iota(jnp.int32, (CHUNK, CHUNK), 1)
    group_lane = lax.broadcasted_iota(jnp.int32, (16, 16), 1) == i // 2
    rate = jnp.sum(jnp.where(group_lane, rates_ref[...], 0.0), axis=1, keepdims=True)
    weight = jnp.sum(jnp.where(group_lane, residue_ref[...], 0.0), axis=1, keepdims=True)
    steps = lax.broadcasted_iota(jnp.int32, (16, CHUNK), 1).astype(f32)
    rate = jnp.broadcast_to(rate, (16, CHUNK))
    weight = jnp.broadcast_to(weight, (16, CHUNK))
    filters = jnp.sum(weight * jnp.exp(-rate * steps), axis=0, keepdims=True)
    rolled = pltpu.roll(jnp.broadcast_to(filters, (CHUNK, CHUNK)), 0, 1, stride=1, stride_axis=0)
    toeplitz = jnp.where(lane >= row, rolled, 0.0).T
    to_end = jnp.exp(-rate * (CHUNK - 1 - steps))
    from_start = weight * jnp.exp(-rate * (steps + 1.0))
    from_start = jnp.concatenate([from_start, jnp.zeros((CHUNK - 16, CHUNK), f32)], axis=0).T

    pick = lax.broadcasted_iota(jnp.int32, (8, 256), 1) == 8 * i + lax.broadcasted_iota(jnp.int32, (8, 256), 0)
    skips = jnp.sum(jnp.where(pick, skip_ref[...], 0.0), axis=1, keepdims=True)
    skips = jnp.broadcast_to(skips, (8, CHUNK))
    for group in range(3):
        for lag in range(7):
            value = jnp.where(pick, taps_ref[group, lag : lag + 1, :], 0.0)
            taps[group, lag] = jnp.broadcast_to(jnp.sum(value, axis=1, keepdims=True), (8, CHUNK))

    @pl.when(c == holder)
    def _():
        pltpu.make_async_copy(ebuf.at[x], ebuf.at[x], recv_sems.at[e_slots[0] + x]).wait()
        for place, copy in emb_relays():
            pltpu.make_async_copy(ebuf.at[place], ebuf.at[place], recv_sems.at[e_slots[0] + place]).wait()
            copy.start()

    @pl.when(c != holder)
    def _():
        for k in range(NX):
            pltpu.make_async_copy(ebuf.at[k], ebuf.at[k], recv_sems.at[e_slots[k]]).wait()

    receive("swap", wo_own)
    for d in (2, 6, 1, 7):
        send("wz" + str(d), wo_own, wo_own, at(zz=(z + d) % NZ))

    for k in range(NY):
        gain = gain_ref[pl.ds(k * NZ + z, 1), :]
        enorm[:, k * 128 : (k + 1) * 128] = (ebuf[k].astype(f32) * gain).astype(bf16)
    for d in range(1, NY):
        receive("w" + str(d), wbuf.at[(y + NY - d) % NY])

    def partial(group):
        weights = jnp.concatenate([wbuf[k, group] for k in range(NY)], axis=1)
        return dot_nt(weights, enorm[...])

    keys, values = partial(1), partial(2)
    for k in range(NZ):
        part = slice(k * 8, (k + 1) * 8)
        send_kv[k] = jnp.concatenate([keys[part], values[part]], axis=0).astype(bf16)
    for d in (4, 3, 5, 2, 6, 1, 7):
        to = (z + d) % NZ
        send("kv" + str(d), send_kv.at[to], arrived_kv.at[z], at(zz=to))
    asks = partial(0)
    for k in range(NZ):
        part = slice(k * 8, (k + 1) * 8)
        send_q[k] = jnp.concatenate([asks[part, 0:256], asks[part, 256:512]], axis=0).astype(bf16)
    for d in (4, 3, 5, 2, 6, 1, 7):
        to = (z + d) % NZ
        send("q" + str(d), send_q.at[to], arrived_q.at[z], at(zz=to))
    own_kv[...] = send_kv[z].astype(f32)
    own_q[...] = send_q[z].astype(f32)

    for d in range(1, NZ):
        receive("tz" + str(d), tokens.at[y, (z + NZ - d) % NZ])
    for d in range(1, NY):
        send("ty" + str(d), tokens.at[y], tokens.at[y], at(yy=(y + d) % NY))

    def wo_place(origin, half=None):
        rows, first = (256, 0) if half is None else (128, half * 128)
        return wo.at[
            pl.ds(aligned(2 * y + origin // share, 256) + first, rows),
            pl.ds(aligned(origin % share, 128), 128),
        ]

    for d in (1, 7, 2, 6):
        receive("wz" + str(d), wo_place((z + NZ - d) % NZ))
    ahead, behind = at(zz=(z + 2) % NZ), at(zz=(z + NZ - 2) % NZ)
    block = wo_place((z + NZ - 1) % NZ)
    send("wz3", block, block, ahead)
    block = wo_place((z + 1) % NZ)
    send("wz5", block, block, behind)
    block = wo_place((z + NZ - 2) % NZ, 0)
    send("wz4a", block, block, ahead)
    block = wo_place((z + 2) % NZ, 1)
    send("wz4b", block, block, behind)

    def along_y(offset):
        block = wo_place((z + offset) % NZ)
        send("wy_up%d" % offset, block, block, at(yy=up))
        send("wy_down%d" % offset, block, block, at(yy=down))

    for offset in (0, 1, 7, 2, 6):
        along_y(offset)

    for d in range(1, NY):
        receive("ty" + str(d), tokens.at[(y + NY - d) % NY])
    for k in range(count_ctx):
        these = tokens[k // NZ, k % NZ]
        token_mat[k * 4 : (k + 1) * 4, :] = (these % 128).astype(f32)
        token_page[k * 4 : (k + 1) * 4, :] = (these // 128).astype(f32)
    token_mat[...] = token_mat[...].T
    token_page[...] = token_page[...].T
    vocab_row = row.astype(f32)

    def mark(n, carry):
        for h in range(2):
            these = token_mat[pl.ds(2 * n + h, 1), :]
            hits = jnp.where(vocab_row == these, 1.0, 0.0)
            one_hot[n, :, h * 128 : (h + 1) * 128] = hits.astype(bf16)
        return carry

    lax.fori_loop(0, 64, mark, 0)

    for d in range(1, count_fsdp):
        receive("sq" + str(d), squares.at[(j + count_fsdp - d) % count_fsdp])
    all_squares = squares[0]
    for k in range(1, count_fsdp):
        all_squares = all_squares + squares[k]
    width = gain_ref.shape[0] * gain_ref.shape[1]
    scale = lax.rsqrt(all_squares * (1.0 / width) + 1e-05)

    value = own_kv[...]
    for d in (1, 7, 2, 6, 3, 5, 4):
        origin = (z + NZ - d) % NZ
        receive("kv" + str(d), arrived_kv.at[origin])
        value = value + arrived_kv[origin].astype(f32)
    table[8:24, :] = value * scale
    value = own_q[...]
    for d in (1, 7, 2, 6, 3, 5, 4):
        origin = (z + NZ - d) % NZ
        receive("q" + str(d), arrived_q.at[origin])
        value = value + arrived_q[origin].astype(f32)
    table[0:8, :] = jnp.concatenate([value[0:8], value[8:16]], axis=1) * scale

    receive("wz3", wo_place((z + NZ - 3) % NZ))
    receive("wz5", wo_place((z + 3) % NZ))
    receive("wz4a", wo_place((z + 4) % NZ, 0))
    receive("wz4b", wo_place((z + 4) % NZ, 1))
    for offset in (3, 5, 4):
        along_y(offset)

    pages = [table[0:24, k * 128 : (k + 1) * 128] for k in range(4)]
    table16 = jnp.concatenate(pages, axis=0).astype(bf16)

    def look_up(n, carry):
        found = dot(table16, one_hot[n])
        for h in range(2):
            page = jnp.broadcast_to(token_page[pl.ds(2 * n + h, 1), :], (24, 128))
            options = [found[k * 24 : (k + 1) * 24, h * 128 : (h + 1) * 128] for k in range(4)]
            low = jnp.where(page == 0.0, options[0], options[1])
            high = jnp.where(page == 2.0, options[2], options[3])
            value = jnp.where(page < 2.0, low, high)
            rows = pl.ds(aligned(2 * n + h + 8, 8), 8)
            for group in range(3):
                short_in[group, rows, :] = value[group * 8 : (group + 1) * 8]
        return carry

    lax.fori_loop(0, 64, look_up, 0, unroll=4)
    for group in range(3):
        tail = short_in[group, 1024:1088, :]
        shifted = pltpu.roll(tail, 1, 1)
        first_lane = lax.broadcasted_iota(jnp.int32, (64, 128), 1) == 0
        short_in[group, 0:64, :] = jnp.where(first_lane, 0.0, shifted)

    def convolve(n, carry):
        sums = []
        for group in range(3):
            result = taps[group, 0] * short_in[group, pl.ds(aligned(n + 8, 8), 8), :]
            for lag in range(1, 7):
                rows = pl.ds(aligned(n + 8 - lag, 8), 8)
                result = result + taps[group, lag] * short_in[group, rows, :]
            sums.append(result)
        here = pl.ds(aligned(n, 8), 8)
        queries[here, :] = sums[0]
        driving[here, :] = sums[1] * sums[2]
        return carry

    lax.fori_loop(0, 128, convolve, 0, unroll=4)

    planes = [driving[pl.ds(k, CHUNK, stride=8), :] for k in range(8)]
    wide = jnp.concatenate(planes, axis=1)
    ends = dot_three(to_end, wide)
    states = jnp.concatenate([ends[:, k * 128 : (k + 1) * 128] for k in range(8)], axis=0)
    rates = jnp.concatenate([rate] * 8, axis=0)

    def later(value, count):
        return jnp.where(lane >= count, pltpu.roll(value, count, 1), 0.0)

    for level in range(7):
        reach = 1 << level
        states = states + jnp.exp(-rates * float(CHUNK * reach)) * later(states, reach)
    states = later(states, 1)
    starts = jnp.concatenate([states[k * 16 : (k + 1) * 16] for k in range(8)], axis=1)
    starts = jnp.concatenate([starts, jnp.zeros((CHUNK - 16, 1024), f32)], axis=0)
    convolved[...] = dot_three(toeplitz, wide) + dot_three(from_start, starts)
    for k in range(8):
        response = convolved[:, k * 128 : (k + 1) * 128] + skips[k : k + 1, :] * planes[k]
        result = queries[pl.ds(k, CHUNK, stride=8), :] * response
        gated_f[pl.ds(k, CHUNK, stride=8), :] = result.T
    gated_b[...] = gated_f[...].astype(bf16)

    def positions(index):
        return gated_b.at[pl.ds(aligned(index, 32), 32), :]

    far = sorted(range(1, count_ctx), key=lambda d: -min(d % NZ, NZ - d % NZ))
    for d in far:
        to = (i + d) % count_ctx
        send("a" + str(d), positions(to), landed.at[i], (to, j))
    landed[i] = gated_b[pl.ds(aligned(i, 32), 32), :]
    for d in reversed(far):
        receive("a" + str(d), landed.at[(i + count_ctx - d) % count_ctx])
    for k in range(4):
        for h in range(2):
            blocks = [landed[n].astype(f32)[k * 8 : (k + 1) * 8] for n in range(h * 16, (h + 1) * 16)]
            block = jnp.concatenate(blocks, axis=0)
            gated[j, k * 128 : (k + 1) * 128, h * 128 : (h + 1) * 128] = block.T.astype(bf16)

    halves = (pl.ds(0, 256), pl.ds(256, 256))
    own = [gated.at[j, half, :] for half in halves]
    send("g_right0", own[0], own[0], at(xx=right))
    send("g_left1", own[1], own[1], at(xx=left))
    send("g_right1", own[1], own[1], at(xx=right))
    send("g_left0", own[0], own[0], at(xx=left))
    send("g_mate", gated.at[j], gated.at[j], at(cc=1 - c))

    def from_y(name, line):
        for offset in range(NZ):
            origin = (z + offset) % NZ
            receive(
                name + str(offset),
                wo.at[
                    pl.ds(aligned(2 * line + origin // share, 256), 256),
                    pl.ds(aligned(origin % share, 128), 128),
                ],
            )

    from_y("wy_up", down)
    block = wo.at[pl.ds(aligned(2 * down, 256), 256), :]
    send("wy_on_up", block, block, at(yy=up))
    from_y("wy_down", up)
    block = wo.at[pl.ds(aligned(2 * up + 1, 256), 256), :]
    send("wy_on_down", block, block, at(yy=down))

    left_j, right_j, across_j = left * NC + c, right * NC + c, across * NC + c
    from_left = [gated.at[left_j, half, :] for half in halves]
    from_right = [gated.at[right_j, half, :] for half in halves]
    from_across = [gated.at[across_j, half, :] for half in halves]
    receive("g_right0", from_left[0])
    send("g_on_right", from_left[0], from_left[0], at(xx=right))
    receive("g_left1", from_right[1])
    send("g_on_left", from_right[1], from_right[1], at(xx=left))
    send("m_left0", from_left[0], from_left[0], mate)
    send("m_right1", from_right[1], from_right[1], mate)
    receive("g_right1", from_left[1])
    send("m_left1", from_left[1], from_left[1], mate)
    receive("g_left0", from_right[0])
    send("m_right0", from_right[0], from_right[0], mate)

    receive("wy_on_up", wo.at[pl.ds(aligned(2 * opposite, 256), 256), :])
    receive("wy_on_down", wo.at[pl.ds(aligned(2 * opposite + 1, 256), 256), :])

    def product(index):
        return dot(gated[index], wo[pl.ds(aligned(index, 256), 256), :])

    mate_j = x * NC + 1 - c
    total[...] = product(j)
    receive("g_mate", gated.at[mate_j])
    total[...] += product(mate_j)
    total[...] += product(left_j)
    total[...] += product(right_j)
    receive("g_on_right", from_across[0])
    send("m_across0", from_across[0], from_across[0], mate)
    receive("g_on_left", from_across[1])
    send("m_across1", from_across[1], from_across[1], mate)
    for name, place in (("left", left), ("right", right), ("across", across)):
        index = place * NC + 1 - c
        if name == "across":
            total[...] += product(across_j)
        receive("m_" + name + "0", gated.at[index, halves[0], :])
        receive("m_" + name + "1", gated.at[index, halves[1], :])
        if name == "across":
            out_ref[...] = (total[...] + product(index)).astype(bf16)
        else:
            total[...] += product(index)

    for copy in sent:
        copy.wait_send()

    @pl.when(c == holder)
    def _():
        for copy in emb_copies():
            copy.wait_send()
        for _, copy in emb_relays():
            copy.wait_send()

    @pl.when(moves)
    def _():
        swap_copy().wait_send()


SEMAPHORES = 180


def body(
    tokens,
    embedding,
    norm_gain,
    in_weight,
    short_taps,
    decay_rates,
    residue,
    skip_weight,
    out_weight,
):
    whole = pl.BlockSpec(memory_space=pltpu.VMEM)
    outside = pl.BlockSpec(memory_space=pl.ANY)
    vm = pltpu.VMEM
    return pl.pallas_call(
        kernel,
        out_shape=jax.ShapeDtypeStruct((512, 512), bf16),
        in_specs=[outside] * 9,
        out_specs=whole,
        scratch_shapes=[
            vm((4, 128), jnp.int32),
            vm((32, 128), f32),
            vm((1, 256), f32),
            vm((3, 7, 256), f32),
            vm((16, 16), f32),
            vm((16, 16), f32),
            vm((3, 128, 256), bf16),
            vm((512, 512), bf16),
            vm((3, 256, 128), bf16),
            vm((NY, 3, 64, 128), bf16),
            vm((NX, 512, 128), bf16),
            vm((512, 512), bf16),
            vm((NX * NC, 1, 512), f32),
            vm((NZ, 16, 512), bf16),
            vm((NZ, 16, 256), bf16),
            vm((NZ, 16, 512), bf16),
            vm((NZ, 16, 256), bf16),
            vm((16, 512), f32),
            vm((16, 256), f32),
            vm((24, 512), f32),
            vm((NY, NZ, 4, 128), jnp.int32),
            vm((128, 128), f32),
            vm((128, 128), f32),
            vm((64, 128, 256), bf16),
            vm((3, 1088, 128), f32),
            vm((3, 7, 8, 128), f32),
            vm((1024, 128), f32),
            vm((1024, 128), f32),
            vm((128, 1024), f32),
            vm((1024, 128), f32),
            vm((1024, 128), bf16),
            vm((NY * NZ, 32, 128), bf16),
            vm((NX * NC, 512, 256), bf16),
            vm((2048, 512), bf16),
            vm((512, 512), f32),
            pltpu.SemaphoreType.DMA((8,)),
            pltpu.SemaphoreType.DMA((SEMAPHORES,)),
            pltpu.SemaphoreType.DMA((SEMAPHORES,)),
        ],
        compiler_params=pltpu.CompilerParams(
            collective_id=0, has_side_effects=True, vmem_limit_bytes=60 * 1024 * 1024
        ),
    )(
        tokens.reshape(4, 128),
        norm_gain.reshape(32, 128),
        skip_weight.reshape(1, 256),
        short_taps.transpose(1, 0, 2),
        decay_rates,
        residue,
        in_weight.transpose(1, 0, 2),
        embedding,
        out_weight,
    )


def solution(mesh):
    placed = (
        P("ctx"),
        P(None, "fsdp"),
        P(),
        P("ctx", None, "fsdp"),
        P(None, None, "fsdp"),
        P(None, "fsdp"),
        P(None, "fsdp"),
        P("fsdp"),
        P("fsdp", "ctx"),
    )
    return jax.shard_map(
        body, mesh=mesh, in_specs=placed, out_specs=P("ctx", "fsdp"), check_vma=False
    )
```

```python
import functools

import jax
import jax.numpy as jnp
from jax import lax
from jax.experimental import pallas as pl
from jax.experimental.pallas import tpu as pltpu
from jax.sharding import PartitionSpec as P

GROUP = 16
CHUNK = 128
NY, NZ, NX, NC = 4, 8, 4, 2
f32 = jnp.float32
bf16 = jnp.bfloat16
MESH = pl.DeviceIdType.MESH


def split(value):
    high = value.astype(bf16)
    return high, (value - high.astype(f32)).astype(bf16)


def dot(a, b):
    return jnp.dot(a, b, preferred_element_type=f32)


def dot_three(a, b):
    a_high, a_low = split(a)
    b_high, b_low = split(b)
    return dot(a_high, b_high) + dot(a_low, b_high) + dot(a_high, b_low)


def dot_nt(a, b):
    return lax.dot_general(a, b, (((1,), (1,)), ((), ())), preferred_element_type=f32)


def aligned(index, size):
    return pl.multiple_of(index * size, size)


def kernel(
    tokens_in,
    gain_in,
    skip_in,
    taps_in,
    rates_in,
    residue_in,
    w_in,
    emb_in,
    ow_ref,
    out_ref,
    tokens_ref,
    gain_ref,
    skip_ref,
    taps_ref,
    rates_ref,
    residue_ref,
    w_ref,
    emb_ref,
    wt,
    wbuf,
    ebuf,
    enorm,
    squares,
    send_kv,
    send_q,
    arrived_kv,
    arrived_q,
    own_kv,
    own_q,
    table,
    tokens,
    token_mat,
    token_page,
    one_hot,
    short_in,
    taps,
    driving,
    queries,
    convolved,
    gated_f,
    gated_b,
    landed,
    gated,
    wo,
    total,
    load_sems,
    send_sems,
    recv_sems,
):
    i = lax.axis_index("ctx")
    j = lax.axis_index("fsdp")
    y, z = i // NZ, i % NZ
    x, c = j // NC, j % NC
    up, down = (y + 1) % NY, (y + NY - 1) % NY
    opposite = (y + 2) % NY
    right, left = (x + 1) % NX, (x + NX - 1) % NX
    across = (x + 2) % NX
    count_ctx = NY * NZ
    count_fsdp = NX * NC
    share = count_ctx // count_fsdp

    def at(yy=None, zz=None, xx=None, cc=None):
        yy = y if yy is None else yy
        zz = z if zz is None else zz
        xx = x if xx is None else xx
        cc = c if cc is None else cc
        return (yy * NZ + zz, xx * NC + cc)

    labels = {}
    sent = []

    def slot(name):
        return labels.setdefault(name, len(labels))

    def remote(name, source, target, device):
        k = slot(name)
        return pltpu.make_async_remote_copy(
            src_ref=source,
            dst_ref=target,
            send_sem=send_sems.at[k],
            recv_sem=recv_sems.at[k],
            device_id=device,
            device_id_type=MESH,
        )

    def send(name, source, target, device):
        copy = remote(name, source, target, device)
        copy.start()
        sent.append(copy)

    def receive(name, target):
        pltpu.make_async_copy(target, target, recv_sems.at[slot(name)]).wait()

    def load(k, source, target):
        copy = pltpu.make_async_copy(source, target, load_sems.at[k])
        copy.start()
        return copy

    emb_load = load(0, emb_in, emb_ref)
    w_load = load(1, w_in, w_ref)
    small_loads = [
        load(2, tokens_in, tokens_ref),
        load(3, gain_in, gain_ref),
        load(4, skip_in, skip_ref),
        load(5, taps_in, taps_ref),
        load(6, rates_in, rates_ref),
        load(7, residue_in, residue_ref),
    ]

    barrier = pltpu.get_barrier_semaphore()

    def greet(device):
        pl.semaphore_signal(barrier, inc=1, device_id=device, device_id_type=MESH)

    for d in range(1, count_ctx):
        greet(((i + d) % count_ctx, j))
    for d in range(1, count_fsdp):
        greet((i, (j + d) % count_fsdp))
    swap_to = (share * j + i % share, i // share)
    moves = jnp.logical_or(swap_to[0] != i, swap_to[1] != j)

    @pl.when(moves)
    def _():
        greet(swap_to)

    w_load.wait()
    for group in range(3):
        for h in range(2):
            block = w_ref[group, :, h * 128 : (h + 1) * 128].astype(f32)
            wt[group, h * 128 : (h + 1) * 128, :] = block.T.astype(bf16)
    for copy in small_loads:
        copy.wait()
    pl.semaphore_wait(barrier, count_ctx - 1 + count_fsdp - 1 + jnp.where(moves, 1, 0))

    wo_rows = pl.ds(aligned(2 * y + z // share, 256), 256)
    wo_cols = pl.ds(aligned(z % share, 128), 128)
    wo_own = wo.at[wo_rows, wo_cols]

    def swap_copy():
        return remote("swap", ow_ref, wo.at[pl.ds(aligned(j, 256), 256), wo_cols], swap_to)

    @pl.when(moves)
    def _():
        swap_copy().start()

    @pl.when(jnp.logical_not(moves))
    def _():
        pltpu.make_async_copy(ow_ref, wo_own, recv_sems.at[slot("swap")]).start()

    emb_load.wait()
    holder = z // share
    e_slots = [slot("e" + str(k)) for k in range(NX)]
    emb_piece = emb_ref.at[:, pl.ds(aligned(z % share, 128), 128)]

    def emb_copy(k, source, place, device):
        return pltpu.make_async_remote_copy(
            src_ref=source,
            dst_ref=ebuf.at[place],
            send_sem=send_sems.at[slot("es" + str(k))],
            recv_sem=recv_sems.at[e_slots[0] + place],
            device_id=device,
            device_id_type=MESH,
        )

    mate = at(cc=1 - c)

    def emb_copies():
        copies = [emb_copy(d, emb_piece, x, at(xx=(x + d) % NX)) for d in (2, 1, 3)]
        return copies + [emb_copy(0, emb_piece, x, mate)]

    def emb_relays():
        places = [(x + d) % NX for d in (1, 3, 2)]
        return [(place, emb_copy(4 + n, ebuf.at[place], place, mate)) for n, place in enumerate(places)]

    @pl.when(c == holder)
    def _():
        for copy in emb_copies():
            copy.start()
        pltpu.make_async_copy(emb_piece, ebuf.at[x], recv_sems.at[e_slots[0] + x]).start()

    def w_rows(to):
        return wt.at[:, pl.ds(aligned(to, 64), 64), :]

    for d in (2, 1, 3):
        to = (y + d) % NY
        send("w" + str(d), w_rows(to), wbuf.at[y], at(yy=to))

    for d in range(1, NZ):
        send("tz" + str(d), tokens_ref, tokens.at[y, z], at(zz=(z + d) % NZ))
    wbuf[y] = wt[:, pl.ds(aligned(y, 64), 64), :]
    tokens[y, z] = tokens_ref[...]

    ones = jnp.ones((8, 512), bf16)
    piece = emb_ref[...].astype(f32)
    high, low = split(piece * piece)
    squares[j] = (dot_nt(ones, high) + dot_nt(ones, low))[0:1, :]

    for d in range(1, count_fsdp):
        send("sq" + str(d), squares.at[j], squares.at[j], (i, (j + d) % count_fsdp))

    row = lax.broadcasted_iota(jnp.int32, (CHUNK, CHUNK), 0)
    lane = lax.broadcasted_iota(jnp.int32, (CHUNK, CHUNK), 1)
    group_lane = lax.broadcasted_iota(jnp.int32, (16, 16), 1) == i // 2
    rate = jnp.sum(jnp.where(group_lane, rates_ref[...], 0.0), axis=1, keepdims=True)
    weight = jnp.sum(jnp.where(group_lane, residue_ref[...], 0.0), axis=1, keepdims=True)
    steps = lax.broadcasted_iota(jnp.int32, (16, CHUNK), 1).astype(f32)
    rate = jnp.broadcast_to(rate, (16, CHUNK))
    weight = jnp.broadcast_to(weight, (16, CHUNK))
    filters = jnp.sum(weight * jnp.exp(-rate * steps), axis=0, keepdims=True)
    rolled = pltpu.roll(jnp.broadcast_to(filters, (CHUNK, CHUNK)), 0, 1, stride=1, stride_axis=0)
    toeplitz = jnp.where(lane >= row, rolled, 0.0).T
    to_end = jnp.exp(-rate * (CHUNK - 1 - steps))
    from_start = weight * jnp.exp(-rate * (steps + 1.0))
    from_start = jnp.concatenate([from_start, jnp.zeros((CHUNK - 16, CHUNK), f32)], axis=0).T

    pick = lax.broadcasted_iota(jnp.int32, (8, 256), 1) == 8 * i + lax.broadcasted_iota(jnp.int32, (8, 256), 0)
    skips = jnp.sum(jnp.where(pick, skip_ref[...], 0.0), axis=1, keepdims=True)
    skips = jnp.broadcast_to(skips, (8, CHUNK))
    for group in range(3):
        for lag in range(7):
            value = jnp.where(pick, taps_ref[group, lag : lag + 1, :], 0.0)
            taps[group, lag] = jnp.broadcast_to(jnp.sum(value, axis=1, keepdims=True), (8, CHUNK))

    receive("swap", wo_own)
    for d in (2, 6, 1, 7):
        send("wz" + str(d), wo_own, wo_own, at(zz=(z + d) % NZ))

    @pl.when(c == holder)
    def _():
        pltpu.make_async_copy(ebuf.at[x], ebuf.at[x], recv_sems.at[e_slots[0] + x]).wait()
        for place, copy in emb_relays():
            pltpu.make_async_copy(ebuf.at[place], ebuf.at[place], recv_sems.at[e_slots[0] + place]).wait()
            copy.start()

    @pl.when(c != holder)
    def _():
        for k in range(NX):
            pltpu.make_async_copy(ebuf.at[k], ebuf.at[k], recv_sems.at[e_slots[k]]).wait()

    for k in range(NY):
        gain = gain_ref[pl.ds(k * NZ + z, 1), :]
        enorm[:, k * 128 : (k + 1) * 128] = (ebuf[k].astype(f32) * gain).astype(bf16)
    for d in range(1, NY):
        receive("w" + str(d), wbuf.at[(y + NY - d) % NY])

    def partial(group):
        weights = jnp.concatenate([wbuf[k, group] for k in range(NY)], axis=1)
        return dot_nt(weights, enorm[...])

    keys, values = partial(1), partial(2)
    for k in range(NZ):
        part = slice(k * 8, (k + 1) * 8)
        send_kv[k] = jnp.concatenate([keys[part], values[part]], axis=0).astype(bf16)
    for d in (4, 3, 5, 2, 6, 1, 7):
        to = (z + d) % NZ
        send("kv" + str(d), send_kv.at[to], arrived_kv.at[z], at(zz=to))
    asks = partial(0)
    for k in range(NZ):
        part = slice(k * 8, (k + 1) * 8)
        send_q[k] = jnp.concatenate([asks[part, 0:256], asks[part, 256:512]], axis=0).astype(bf16)
    for d in (4, 3, 5, 2, 6, 1, 7):
        to = (z + d) % NZ
        send("q" + str(d), send_q.at[to], arrived_q.at[z], at(zz=to))
    own_kv[...] = send_kv[z].astype(f32)
    own_q[...] = send_q[z].astype(f32)

    for d in range(1, NZ):
        receive("tz" + str(d), tokens.at[y, (z + NZ - d) % NZ])
    for d in range(1, NY):
        send("ty" + str(d), tokens.at[y], tokens.at[y], at(yy=(y + d) % NY))

    for d in range(1, NY):
        receive("ty" + str(d), tokens.at[(y + NY - d) % NY])
    for k in range(count_ctx):
        these = tokens[k // NZ, k % NZ]
        token_mat[k * 4 : (k + 1) * 4, :] = (these % 128).astype(f32)
        token_page[k * 4 : (k + 1) * 4, :] = (these // 128).astype(f32)
    token_mat[...] = token_mat[...].T
    token_page[...] = token_page[...].T
    def wo_place(origin, half=None):
        rows, first = (256, 0) if half is None else (128, half * 128)
        return wo.at[
            pl.ds(aligned(2 * y + origin // share, 256) + first, rows),
            pl.ds(aligned(origin % share, 128), 128),
        ]

    for d in (1, 7, 2, 6):
        receive("wz" + str(d), wo_place((z + NZ - d) % NZ))
    def along_y(offset):
        block = wo_place((z + offset) % NZ)
        send("wy_up%d" % offset, block, block, at(yy=up))
        send("wy_down%d" % offset, block, block, at(yy=down))

    for offset in (0, 1, 7, 2, 6):
        along_y(offset)

    vocab_row = row.astype(f32)

    def mark(n, carry):
        for h in range(2):
            these = token_mat[pl.ds(2 * n + h, 1), :]
            hits = jnp.where(vocab_row == these, 1.0, 0.0)
            one_hot[n, :, h * 128 : (h + 1) * 128] = hits.astype(bf16)
        return carry

    lax.fori_loop(0, 64, mark, 0)

    for d in range(1, count_fsdp):
        receive("sq" + str(d), squares.at[(j + count_fsdp - d) % count_fsdp])
    all_squares = squares[0]
    for k in range(1, count_fsdp):
        all_squares = all_squares + squares[k]
    width = gain_ref.shape[0] * gain_ref.shape[1]
    scale = lax.rsqrt(all_squares * (1.0 / width) + 1e-05)

    value = own_kv[...]
    for d in (1, 7, 2, 6, 3, 5, 4):
        origin = (z + NZ - d) % NZ
        receive("kv" + str(d), arrived_kv.at[origin])
        value = value + arrived_kv[origin].astype(f32)
    table[8:24, :] = value * scale
    value = own_q[...]
    for d in (1, 7, 2, 6, 3, 5, 4):
        origin = (z + NZ - d) % NZ
        receive("q" + str(d), arrived_q.at[origin])
        value = value + arrived_q[origin].astype(f32)
    table[0:8, :] = jnp.concatenate([value[0:8], value[8:16]], axis=1) * scale

    ahead, behind = at(zz=(z + 2) % NZ), at(zz=(z + NZ - 2) % NZ)
    block = wo_place((z + NZ - 1) % NZ)
    send("wz3", block, block, ahead)
    block = wo_place((z + 1) % NZ)
    send("wz5", block, block, behind)
    block = wo_place((z + NZ - 2) % NZ, 0)
    send("wz4a", block, block, ahead)
    block = wo_place((z + 2) % NZ, 1)
    send("wz4b", block, block, behind)

    pages = [table[0:24, k * 128 : (k + 1) * 128] for k in range(4)]
    table16 = jnp.concatenate(pages, axis=0).astype(bf16)

    def look_up(n, carry):
        found = dot(table16, one_hot[n])
        for h in range(2):
            page = jnp.broadcast_to(token_page[pl.ds(2 * n + h, 1), :], (24, 128))
            options = [found[k * 24 : (k + 1) * 24, h * 128 : (h + 1) * 128] for k in range(4)]
            low = jnp.where(page == 0.0, options[0], options[1])
            high = jnp.where(page == 2.0, options[2], options[3])
            value = jnp.where(page < 2.0, low, high)
            rows = pl.ds(aligned(2 * n + h + 8, 8), 8)
            for group in range(3):
                short_in[group, rows, :] = value[group * 8 : (group + 1) * 8]
        return carry

    lax.fori_loop(0, 64, look_up, 0, unroll=4)
    for group in range(3):
        tail = short_in[group, 1024:1088, :]
        shifted = pltpu.roll(tail, 1, 1)
        first_lane = lax.broadcasted_iota(jnp.int32, (64, 128), 1) == 0
        short_in[group, 0:64, :] = jnp.where(first_lane, 0.0, shifted)

    def convolve(n, carry):
        sums = []
        for group in range(3):
            result = taps[group, 0] * short_in[group, pl.ds(aligned(n + 8, 8), 8), :]
            for lag in range(1, 7):
                rows = pl.ds(aligned(n + 8 - lag, 8), 8)
                result = result + taps[group, lag] * short_in[group, rows, :]
            sums.append(result)
        here = pl.ds(aligned(n, 8), 8)
        queries[here, :] = sums[0]
        driving[here, :] = sums[1] * sums[2]
        return carry

    lax.fori_loop(0, 128, convolve, 0, unroll=4)

    planes = [driving[pl.ds(k, CHUNK, stride=8), :] for k in range(8)]
    wide = jnp.concatenate(planes, axis=1)
    ends = dot_three(to_end, wide)
    states = jnp.concatenate([ends[:, k * 128 : (k + 1) * 128] for k in range(8)], axis=0)
    rates = jnp.concatenate([rate] * 8, axis=0)

    def later(value, count):
        return jnp.where(lane >= count, pltpu.roll(value, count, 1), 0.0)

    for level in range(7):
        reach = 1 << level
        states = states + jnp.exp(-rates * float(CHUNK * reach)) * later(states, reach)
    states = later(states, 1)
    starts = jnp.concatenate([states[k * 16 : (k + 1) * 16] for k in range(8)], axis=1)
    starts = jnp.concatenate([starts, jnp.zeros((CHUNK - 16, 1024), f32)], axis=0)
    convolved[...] = dot_three(toeplitz, wide) + dot_three(from_start, starts)
    for k in range(8):
        response = convolved[:, k * 128 : (k + 1) * 128] + skips[k : k + 1, :] * planes[k]
        result = queries[pl.ds(k, CHUNK, stride=8), :] * response
        gated_f[pl.ds(k, CHUNK, stride=8), :] = result.T
    gated_b[...] = gated_f[...].astype(bf16)

    far = sorted(range(1, count_ctx), key=lambda d: -min(d % NZ, NZ - d % NZ))
    for part in range(2):
        for d in far:
            to = (i + d) % count_ctx
            rows = pl.ds(aligned(2 * to + part, 16), 16)
            send("a%d_%d" % (part, d), gated_b.at[rows, :], landed.at[i, pl.ds(16 * part, 16), :], (to, j))
    receive("wz3", wo_place((z + NZ - 3) % NZ))
    receive("wz5", wo_place((z + 3) % NZ))
    receive("wz4a", wo_place((z + 4) % NZ, 0))
    receive("wz4b", wo_place((z + 4) % NZ, 1))
    for offset in (3, 5, 4):
        along_y(offset)

    landed[i] = gated_b[pl.ds(aligned(i, 32), 32), :]

    left_j, right_j, across_j = left * NC + c, right * NC + c, across * NC + c
    mate_j = x * NC + 1 - c
    to_right, to_left = at(xx=right), at(xx=left)

    def quarter(index, k):
        return gated.at[index, pl.ds(128 * k, 128), :]

    def half(index, part):
        return gated.at[index, pl.ds(256 * part, 256), :]

    early = len(sent)
    for part in range(2):
        for d in reversed(far):
            origin = (i + count_ctx - d) % count_ctx
            receive("a%d_%d" % (part, d), landed.at[origin, pl.ds(16 * part, 16), :])
        blocks = [landed[n, part * 16 : part * 16 + 16, :].astype(f32) for n in range(count_ctx)]
        for k in range(2):
            for h in range(2):
                block = [blocks[n][k * 8 : (k + 1) * 8] for n in range(h * 16, (h + 1) * 16)]
                block = jnp.concatenate(block, axis=0)
                rows = slice((2 * part + k) * 128, (2 * part + k + 1) * 128)
                gated[j, rows, h * 128 : (h + 1) * 128] = block.T.astype(bf16)
        first, second = 2 * part, 2 * part + 1
        send("g_right%d" % first, quarter(j, first), quarter(j, first), to_right)
        send("g_left%d" % second, quarter(j, second), quarter(j, second), to_left)
        send("g_right%d" % second, quarter(j, second), quarter(j, second), to_right)
        send("g_left%d" % first, quarter(j, first), quarter(j, first), to_left)
        send("g_mate%d" % part, half(j, part), half(j, part), mate)

    def relay_x(part):
        first, second = 2 * part, 2 * part + 1
        receive("g_right%d" % first, quarter(left_j, first))
        send("g_on_right%d" % part, quarter(left_j, first), quarter(left_j, first), to_right)
        receive("g_left%d" % second, quarter(right_j, second))
        send("g_on_left%d" % part, quarter(right_j, second), quarter(right_j, second), to_left)
        receive("g_right%d" % second, quarter(left_j, second))
        send("m_left%d" % part, half(left_j, part), half(left_j, part), mate)
        receive("g_left%d" % first, quarter(right_j, first))
        send("m_right%d" % part, half(right_j, part), half(right_j, part), mate)

    def from_y(name, line):
        for offset in range(NZ):
            origin = (z + offset) % NZ
            receive(
                name + str(offset),
                wo.at[
                    pl.ds(aligned(2 * line + origin // share, 256), 256),
                    pl.ds(aligned(origin % share, 128), 128),
                ],
            )

    from_y("wy_up", down)
    block = wo.at[pl.ds(aligned(2 * down, 256), 256), :]
    send("wy_on_up", block, block, at(yy=up))
    from_y("wy_down", up)
    block = wo.at[pl.ds(aligned(2 * up + 1, 256), 256), :]
    send("wy_on_down", block, block, at(yy=down))

    relay_x(0)

    relay_x(1)

    def product(index):
        return dot(gated[index], wo[pl.ds(aligned(index, 256), 256), :])

    for copy in sent[:early]:
        copy.wait_send()

    @pl.when(c == holder)
    def _():
        for copy in emb_copies():
            copy.wait_send()
        for _, copy in emb_relays():
            copy.wait_send()

    @pl.when(moves)
    def _():
        swap_copy().wait_send()

    receive("wy_on_up", wo.at[pl.ds(aligned(2 * opposite, 256), 256), :])
    receive("wy_on_down", wo.at[pl.ds(aligned(2 * opposite + 1, 256), 256), :])
    total[...] = product(j)
    total[...] += product(left_j)
    for part in range(2):
        receive("g_on_right%d" % part, quarter(across_j, 2 * part))
        receive("g_on_left%d" % part, quarter(across_j, 2 * part + 1))
        send("m_across%d" % part, half(across_j, part), half(across_j, part), mate)
        if part == 0:
            total[...] += product(right_j)
    receive("g_mate0", half(mate_j, 0))
    receive("g_mate1", half(mate_j, 1))
    total[...] += product(mate_j)
    for name, place in (("left", left), ("right", right), ("across", across)):
        index = place * NC + 1 - c
        if name == "across":
            total[...] += product(across_j)
        receive("m_" + name + "0", half(index, 0))
        receive("m_" + name + "1", half(index, 1))
        if name == "across":
            out_ref[...] = (total[...] + product(index)).astype(bf16)
        else:
            total[...] += product(index)

    for copy in sent[early:]:
        copy.wait_send()


SEMAPHORES = 240


def body(
    tokens,
    embedding,
    norm_gain,
    in_weight,
    short_taps,
    decay_rates,
    residue,
    skip_weight,
    out_weight,
):
    whole = pl.BlockSpec(memory_space=pltpu.VMEM)
    outside = pl.BlockSpec(memory_space=pl.ANY)
    vm = pltpu.VMEM
    return pl.pallas_call(
        kernel,
        out_shape=jax.ShapeDtypeStruct((512, 512), bf16),
        in_specs=[outside] * 9,
        out_specs=whole,
        scratch_shapes=[
            vm((4, 128), jnp.int32),
            vm((32, 128), f32),
            vm((1, 256), f32),
            vm((3, 7, 256), f32),
            vm((16, 16), f32),
            vm((16, 16), f32),
            vm((3, 128, 256), bf16),
            vm((512, 512), bf16),
            vm((3, 256, 128), bf16),
            vm((NY, 3, 64, 128), bf16),
            vm((NX, 512, 128), bf16),
            vm((512, 512), bf16),
            vm((NX * NC, 1, 512), f32),
            vm((NZ, 16, 512), bf16),
            vm((NZ, 16, 256), bf16),
            vm((NZ, 16, 512), bf16),
            vm((NZ, 16, 256), bf16),
            vm((16, 512), f32),
            vm((16, 256), f32),
            vm((24, 512), f32),
            vm((NY, NZ, 4, 128), jnp.int32),
            vm((128, 128), f32),
            vm((128, 128), f32),
            vm((64, 128, 256), bf16),
            vm((3, 1088, 128), f32),
            vm((3, 7, 8, 128), f32),
            vm((1024, 128), f32),
            vm((1024, 128), f32),
            vm((128, 1024), f32),
            vm((1024, 128), f32),
            vm((1024, 128), bf16),
            vm((NY * NZ, 32, 128), bf16),
            vm((NX * NC, 512, 256), bf16),
            vm((2048, 512), bf16),
            vm((512, 512), f32),
            pltpu.SemaphoreType.DMA((8,)),
            pltpu.SemaphoreType.DMA((SEMAPHORES,)),
            pltpu.SemaphoreType.DMA((SEMAPHORES,)),
        ],
        compiler_params=pltpu.CompilerParams(
            collective_id=0, has_side_effects=True, vmem_limit_bytes=60 * 1024 * 1024
        ),
    )(
        tokens.reshape(4, 128),
        norm_gain.reshape(32, 128),
        skip_weight.reshape(1, 256),
        short_taps.transpose(1, 0, 2),
        decay_rates,
        residue,
        in_weight.transpose(1, 0, 2),
        embedding,
        out_weight,
    )


def solution(mesh):
    placed = (
        P("ctx"),
        P(None, "fsdp"),
        P(),
        P("ctx", None, "fsdp"),
        P(None, None, "fsdp"),
        P(None, "fsdp"),
        P(None, "fsdp"),
        P("fsdp"),
        P("fsdp", "ctx"),
    )
    return jax.shard_map(
        body, mesh=mesh, in_specs=placed, out_specs=P("ctx", "fsdp"), check_vma=False
    )
```

```python
import functools

import jax
import jax.numpy as jnp
from jax import lax
from jax.experimental import pallas as pl
from jax.experimental.pallas import tpu as pltpu
from jax.sharding import PartitionSpec as P

GROUP = 16
CHUNK = 128
NY, NZ, NX, NC = 4, 8, 4, 2
f32 = jnp.float32
bf16 = jnp.bfloat16
MESH = pl.DeviceIdType.MESH


def split(value):
    high = value.astype(bf16)
    return high, (value - high.astype(f32)).astype(bf16)


def dot(a, b):
    return jnp.dot(a, b, preferred_element_type=f32)


def dot_three(a, b):
    a_high, a_low = split(a)
    b_high, b_low = split(b)
    return dot(a_high, b_high) + dot(a_low, b_high) + dot(a_high, b_low)


def dot_nt(a, b):
    return lax.dot_general(a, b, (((1,), (1,)), ((), ())), preferred_element_type=f32)


def aligned(index, size):
    return pl.multiple_of(index * size, size)


def kernel(
    tokens_in,
    gain_in,
    skip_in,
    taps_in,
    rates_in,
    residue_in,
    w_in,
    emb_in,
    ow_ref,
    out_ref,
    tokens_ref,
    gain_ref,
    skip_ref,
    taps_ref,
    rates_ref,
    residue_ref,
    w_ref,
    emb_ref,
    wt,
    wbuf,
    ebuf,
    enorm,
    squares,
    send_kv,
    send_q,
    arrived_kv,
    arrived_q,
    own_kv,
    own_q,
    table,
    tokens,
    token_mat,
    token_page,
    one_hot,
    short_in,
    taps,
    driving,
    queries,
    convolved,
    gated_f,
    gated_b,
    landed,
    gated,
    wo,
    total,
    load_sems,
    send_sems,
    recv_sems,
):
    i = lax.axis_index("ctx")
    j = lax.axis_index("fsdp")
    y, z = i // NZ, i % NZ
    x, c = j // NC, j % NC
    up, down = (y + 1) % NY, (y + NY - 1) % NY
    opposite = (y + 2) % NY
    right, left = (x + 1) % NX, (x + NX - 1) % NX
    across = (x + 2) % NX
    count_ctx = NY * NZ
    count_fsdp = NX * NC
    share = count_ctx // count_fsdp

    def at(yy=None, zz=None, xx=None, cc=None):
        yy = y if yy is None else yy
        zz = z if zz is None else zz
        xx = x if xx is None else xx
        cc = c if cc is None else cc
        return (yy * NZ + zz, xx * NC + cc)

    labels = {}
    sent = []

    def slot(name):
        return labels.setdefault(name, len(labels))

    def remote(name, source, target, device):
        k = slot(name)
        return pltpu.make_async_remote_copy(
            src_ref=source,
            dst_ref=target,
            send_sem=send_sems.at[k],
            recv_sem=recv_sems.at[k],
            device_id=device,
            device_id_type=MESH,
        )

    def send(name, source, target, device):
        copy = remote(name, source, target, device)
        copy.start()
        sent.append(copy)

    def receive(name, target):
        pltpu.make_async_copy(target, target, recv_sems.at[slot(name)]).wait()

    def load(k, source, target):
        copy = pltpu.make_async_copy(source, target, load_sems.at[k])
        copy.start()
        return copy

    emb_load = load(0, emb_in, emb_ref)
    w_load = load(1, w_in, w_ref)
    small_loads = [
        load(2, tokens_in, tokens_ref),
        load(3, gain_in, gain_ref),
        load(4, skip_in, skip_ref),
        load(5, taps_in, taps_ref),
        load(6, rates_in, rates_ref),
        load(7, residue_in, residue_ref),
    ]

    barrier = pltpu.get_barrier_semaphore()

    def greet(device):
        pl.semaphore_signal(barrier, inc=1, device_id=device, device_id_type=MESH)

    for d in range(1, NZ):
        greet(at(zz=(z + d) % NZ))
    for d in range(1, NY):
        greet(at(yy=(y + d) % NY))
    for d in range(1, count_fsdp):
        greet((i, (j + d) % count_fsdp))
    swap_to = (share * j + i % share, i // share)
    moves = jnp.logical_or(swap_to[0] != i, swap_to[1] != j)

    @pl.when(moves)
    def _():
        greet(swap_to)

    w_load.wait()
    for group in range(3):
        for h in range(2):
            block = w_ref[group, :, h * 128 : (h + 1) * 128].astype(f32)
            wt[group, h * 128 : (h + 1) * 128, :] = block.T.astype(bf16)
    for copy in small_loads:
        copy.wait()
    pl.semaphore_wait(barrier, NZ - 1 + NY - 1 + count_fsdp - 1 + jnp.where(moves, 1, 0))

    wo_rows = pl.ds(aligned(2 * y + z // share, 256), 256)
    wo_cols = pl.ds(aligned(z % share, 128), 128)
    wo_own = wo.at[wo_rows, wo_cols]

    def swap_copy():
        return remote("swap", ow_ref, wo.at[pl.ds(aligned(j, 256), 256), wo_cols], swap_to)

    @pl.when(moves)
    def _():
        swap_copy().start()

    @pl.when(jnp.logical_not(moves))
    def _():
        pltpu.make_async_copy(ow_ref, wo_own, recv_sems.at[slot("swap")]).start()

    emb_load.wait()
    holder = z // share
    e_slots = [slot("e" + str(k)) for k in range(NX)]
    emb_piece = emb_ref.at[:, pl.ds(aligned(z % share, 128), 128)]

    def emb_copy(k, source, place, device):
        return pltpu.make_async_remote_copy(
            src_ref=source,
            dst_ref=ebuf.at[place],
            send_sem=send_sems.at[slot("es" + str(k))],
            recv_sem=recv_sems.at[e_slots[0] + place],
            device_id=device,
            device_id_type=MESH,
        )

    mate = at(cc=1 - c)

    def emb_copies():
        copies = [emb_copy(d, emb_piece, x, at(xx=(x + d) % NX)) for d in (2, 1, 3)]
        return copies + [emb_copy(0, emb_piece, x, mate)]

    def emb_relays():
        places = [(x + d) % NX for d in (1, 3, 2)]
        return [(place, emb_copy(4 + n, ebuf.at[place], place, mate)) for n, place in enumerate(places)]

    @pl.when(c == holder)
    def _():
        for copy in emb_copies():
            copy.start()
        pltpu.make_async_copy(emb_piece, ebuf.at[x], recv_sems.at[e_slots[0] + x]).start()

    def w_rows(to):
        return wt.at[:, pl.ds(aligned(to, 64), 64), :]

    for d in (2, 1, 3):
        to = (y + d) % NY
        send("w" + str(d), w_rows(to), wbuf.at[y], at(yy=to))

    for d in range(1, NZ):
        send("tz" + str(d), tokens_ref, tokens.at[y, z], at(zz=(z + d) % NZ))
    wbuf[y] = wt[:, pl.ds(aligned(y, 64), 64), :]
    tokens[y, z] = tokens_ref[...]

    ones = jnp.ones((8, 512), bf16)
    piece = emb_ref[...].astype(f32)
    high, low = split(piece * piece)
    squares[j] = (dot_nt(ones, high) + dot_nt(ones, low))[0:1, :]

    for d in range(1, count_fsdp):
        send("sq" + str(d), squares.at[j], squares.at[j], (i, (j + d) % count_fsdp))

    row = lax.broadcasted_iota(jnp.int32, (CHUNK, CHUNK), 0)
    lane = lax.broadcasted_iota(jnp.int32, (CHUNK, CHUNK), 1)
    group_lane = lax.broadcasted_iota(jnp.int32, (16, 16), 1) == i // 2
    rate = jnp.sum(jnp.where(group_lane, rates_ref[...], 0.0), axis=1, keepdims=True)
    weight = jnp.sum(jnp.where(group_lane, residue_ref[...], 0.0), axis=1, keepdims=True)
    steps = lax.broadcasted_iota(jnp.int32, (16, CHUNK), 1).astype(f32)
    rate = jnp.broadcast_to(rate, (16, CHUNK))
    weight = jnp.broadcast_to(weight, (16, CHUNK))
    filters = jnp.sum(weight * jnp.exp(-rate * steps), axis=0, keepdims=True)
    rolled = pltpu.roll(jnp.broadcast_to(filters, (CHUNK, CHUNK)), 0, 1, stride=1, stride_axis=0)
    toeplitz = jnp.where(lane >= row, rolled, 0.0).T
    to_end = jnp.exp(-rate * (CHUNK - 1 - steps))
    from_start = weight * jnp.exp(-rate * (steps + 1.0))
    from_start = jnp.concatenate([from_start, jnp.zeros((CHUNK - 16, CHUNK), f32)], axis=0).T

    pick = lax.broadcasted_iota(jnp.int32, (8, 256), 1) == 8 * i + lax.broadcasted_iota(jnp.int32, (8, 256), 0)
    skips = jnp.sum(jnp.where(pick, skip_ref[...], 0.0), axis=1, keepdims=True)
    skips = jnp.broadcast_to(skips, (8, CHUNK))
    for group in range(3):
        for lag in range(7):
            value = jnp.where(pick, taps_ref[group, lag : lag + 1, :], 0.0)
            taps[group, lag] = jnp.broadcast_to(jnp.sum(value, axis=1, keepdims=True), (8, CHUNK))

    receive("swap", wo_own)
    for d in (2, 6, 1, 7):
        send("wz" + str(d), wo_own, wo_own, at(zz=(z + d) % NZ))

    @pl.when(c == holder)
    def _():
        pltpu.make_async_copy(ebuf.at[x], ebuf.at[x], recv_sems.at[e_slots[0] + x]).wait()
        for place, copy in emb_relays():
            pltpu.make_async_copy(ebuf.at[place], ebuf.at[place], recv_sems.at[e_slots[0] + place]).wait()
            copy.start()

    @pl.when(c != holder)
    def _():
        for k in range(NX):
            pltpu.make_async_copy(ebuf.at[k], ebuf.at[k], recv_sems.at[e_slots[k]]).wait()

    for k in range(NY):
        gain = gain_ref[pl.ds(k * NZ + z, 1), :]
        enorm[:, k * 128 : (k + 1) * 128] = (ebuf[k].astype(f32) * gain).astype(bf16)
    for d in range(1, NY):
        receive("w" + str(d), wbuf.at[(y + NY - d) % NY])

    def partial(group):
        weights = jnp.concatenate([wbuf[k, group] for k in range(NY)], axis=1)
        return dot_nt(weights, enorm[...])

    keys, values = partial(1), partial(2)
    for k in range(NZ):
        part = slice(k * 8, (k + 1) * 8)
        send_kv[k] = jnp.concatenate([keys[part], values[part]], axis=0).astype(bf16)
    for d in (4, 3, 5, 2, 6, 1, 7):
        to = (z + d) % NZ
        send("kv" + str(d), send_kv.at[to], arrived_kv.at[z], at(zz=to))
    asks = partial(0)
    for k in range(NZ):
        part = slice(k * 8, (k + 1) * 8)
        send_q[k] = jnp.concatenate([asks[part, 0:256], asks[part, 256:512]], axis=0).astype(bf16)
    for d in (4, 3, 5, 2, 6, 1, 7):
        to = (z + d) % NZ
        send("q" + str(d), send_q.at[to], arrived_q.at[z], at(zz=to))
    own_kv[...] = send_kv[z].astype(f32)
    own_q[...] = send_q[z].astype(f32)

    for d in range(1, NZ):
        receive("tz" + str(d), tokens.at[y, (z + NZ - d) % NZ])
    for d in range(1, NY):
        send("ty" + str(d), tokens.at[y], tokens.at[y], at(yy=(y + d) % NY))

    for d in range(1, NY):
        receive("ty" + str(d), tokens.at[(y + NY - d) % NY])
    for k in range(count_ctx):
        these = tokens[k // NZ, k % NZ]
        token_mat[k * 4 : (k + 1) * 4, :] = (these % 128).astype(f32)
        token_page[k * 4 : (k + 1) * 4, :] = (these // 128).astype(f32)
    token_mat[...] = token_mat[...].T
    token_page[...] = token_page[...].T
    def wo_place(origin, half=None):
        rows, first = (256, 0) if half is None else (128, half * 128)
        return wo.at[
            pl.ds(aligned(2 * y + origin // share, 256) + first, rows),
            pl.ds(aligned(origin % share, 128), 128),
        ]

    for d in (1, 7, 2, 6):
        receive("wz" + str(d), wo_place((z + NZ - d) % NZ))
    def along_y(offset):
        block = wo_place((z + offset) % NZ)
        send("wy_up%d" % offset, block, block, at(yy=up))
        send("wy_down%d" % offset, block, block, at(yy=down))

    for offset in (0, 1, 7, 2, 6):
        along_y(offset)

    vocab_row = row.astype(f32)

    def mark(n, carry):
        for h in range(2):
            these = token_mat[pl.ds(2 * n + h, 1), :]
            hits = jnp.where(vocab_row == these, 1.0, 0.0)
            one_hot[n, :, h * 128 : (h + 1) * 128] = hits.astype(bf16)
        return carry

    lax.fori_loop(0, 64, mark, 0)

    for d in range(1, count_fsdp):
        receive("sq" + str(d), squares.at[(j + count_fsdp - d) % count_fsdp])
    all_squares = squares[0]
    for k in range(1, count_fsdp):
        all_squares = all_squares + squares[k]
    width = gain_ref.shape[0] * gain_ref.shape[1]
    scale = lax.rsqrt(all_squares * (1.0 / width) + 1e-05)

    value = own_kv[...]
    for d in (1, 7, 2, 6, 3, 5, 4):
        origin = (z + NZ - d) % NZ
        receive("kv" + str(d), arrived_kv.at[origin])
        value = value + arrived_kv[origin].astype(f32)
    table[8:24, :] = value * scale
    value = own_q[...]
    for d in (1, 7, 2, 6, 3, 5, 4):
        origin = (z + NZ - d) % NZ
        receive("q" + str(d), arrived_q.at[origin])
        value = value + arrived_q[origin].astype(f32)
    table[0:8, :] = jnp.concatenate([value[0:8], value[8:16]], axis=1) * scale

    ahead, behind = at(zz=(z + 2) % NZ), at(zz=(z + NZ - 2) % NZ)
    block = wo_place((z + NZ - 1) % NZ)
    send("wz3", block, block, ahead)
    block = wo_place((z + 1) % NZ)
    send("wz5", block, block, behind)
    block = wo_place((z + NZ - 2) % NZ, 0)
    send("wz4a", block, block, ahead)
    block = wo_place((z + 2) % NZ, 1)
    send("wz4b", block, block, behind)

    pages = [table[0:24, k * 128 : (k + 1) * 128] for k in range(4)]
    table16 = jnp.concatenate(pages, axis=0).astype(bf16)

    def look_up(n, carry):
        found = dot(table16, one_hot[n])
        for h in range(2):
            page = jnp.broadcast_to(token_page[pl.ds(2 * n + h, 1), :], (24, 128))
            options = [found[k * 24 : (k + 1) * 24, h * 128 : (h + 1) * 128] for k in range(4)]
            low = jnp.where(page == 0.0, options[0], options[1])
            high = jnp.where(page == 2.0, options[2], options[3])
            value = jnp.where(page < 2.0, low, high)
            rows = pl.ds(aligned(2 * n + h + 8, 8), 8)
            for group in range(3):
                short_in[group, rows, :] = value[group * 8 : (group + 1) * 8]
        return carry

    lax.fori_loop(0, 64, look_up, 0, unroll=4)
    for group in range(3):
        tail = short_in[group, 1024:1088, :]
        shifted = pltpu.roll(tail, 1, 1)
        first_lane = lax.broadcasted_iota(jnp.int32, (64, 128), 1) == 0
        short_in[group, 0:64, :] = jnp.where(first_lane, 0.0, shifted)

    def convolve(n, carry):
        sums = []
        for group in range(3):
            result = taps[group, 0] * short_in[group, pl.ds(aligned(n + 8, 8), 8), :]
            for lag in range(1, 7):
                rows = pl.ds(aligned(n + 8 - lag, 8), 8)
                result = result + taps[group, lag] * short_in[group, rows, :]
            sums.append(result)
        here = pl.ds(aligned(n, 8), 8)
        queries[here, :] = sums[0]
        driving[here, :] = sums[1] * sums[2]
        return carry

    lax.fori_loop(0, 128, convolve, 0, unroll=4)

    planes = [driving[pl.ds(k, CHUNK, stride=8), :] for k in range(8)]
    wide = jnp.concatenate(planes, axis=1)
    ends = dot_three(to_end, wide)
    states = jnp.concatenate([ends[:, k * 128 : (k + 1) * 128] for k in range(8)], axis=0)
    rates = jnp.concatenate([rate] * 8, axis=0)

    def later(value, count):
        return jnp.where(lane >= count, pltpu.roll(value, count, 1), 0.0)

    for level in range(7):
        reach = 1 << level
        states = states + jnp.exp(-rates * float(CHUNK * reach)) * later(states, reach)
    states = later(states, 1)
    starts = jnp.concatenate([states[k * 16 : (k + 1) * 16] for k in range(8)], axis=1)
    starts = jnp.concatenate([starts, jnp.zeros((CHUNK - 16, 1024), f32)], axis=0)
    convolved[...] = dot_three(toeplitz, wide) + dot_three(from_start, starts)
    for k in range(8):
        response = convolved[:, k * 128 : (k + 1) * 128] + skips[k : k + 1, :] * planes[k]
        result = queries[pl.ds(k, CHUNK, stride=8), :] * response
        gated_f[pl.ds(k, CHUNK, stride=8), :] = result.T
    gated_b[...] = gated_f[...].astype(bf16)

    far = sorted(range(1, count_ctx), key=lambda d: -min(d % NZ, NZ - d % NZ))
    for part in range(2):
        for d in far:
            to = (i + d) % count_ctx
            rows = pl.ds(aligned(2 * to + part, 16), 16)
            send("a%d_%d" % (part, d), gated_b.at[rows, :], landed.at[i, pl.ds(16 * part, 16), :], (to, j))
    receive("wz3", wo_place((z + NZ - 3) % NZ))
    receive("wz5", wo_place((z + 3) % NZ))
    receive("wz4a", wo_place((z + 4) % NZ, 0))
    receive("wz4b", wo_place((z + 4) % NZ, 1))
    for offset in (3, 5, 4):
        along_y(offset)

    landed[i] = gated_b[pl.ds(aligned(i, 32), 32), :]

    left_j, right_j, across_j = left * NC + c, right * NC + c, across * NC + c
    mate_j = x * NC + 1 - c
    to_right, to_left = at(xx=right), at(xx=left)

    def quarter(index, k):
        return gated.at[index, pl.ds(128 * k, 128), :]

    def half(index, part):
        return gated.at[index, pl.ds(256 * part, 256), :]

    early = len(sent)
    for part in range(2):
        for d in reversed(far):
            origin = (i + count_ctx - d) % count_ctx
            receive("a%d_%d" % (part, d), landed.at[origin, pl.ds(16 * part, 16), :])
        blocks = [landed[n, part * 16 : part * 16 + 16, :].astype(f32) for n in range(count_ctx)]
        for k in range(2):
            for h in range(2):
                block = [blocks[n][k * 8 : (k + 1) * 8] for n in range(h * 16, (h + 1) * 16)]
                block = jnp.concatenate(block, axis=0)
                rows = slice((2 * part + k) * 128, (2 * part + k + 1) * 128)
                gated[j, rows, h * 128 : (h + 1) * 128] = block.T.astype(bf16)
        first, second = 2 * part, 2 * part + 1
        send("g_right%d" % first, quarter(j, first), quarter(j, first), to_right)
        send("g_left%d" % second, quarter(j, second), quarter(j, second), to_left)
        send("g_right%d" % second, quarter(j, second), quarter(j, second), to_right)
        send("g_left%d" % first, quarter(j, first), quarter(j, first), to_left)
        send("g_mate%d" % part, half(j, part), half(j, part), mate)

    def relay_x(part):
        first, second = 2 * part, 2 * part + 1
        receive("g_right%d" % first, quarter(left_j, first))
        send("g_on_right%d" % part, quarter(left_j, first), quarter(left_j, first), to_right)
        receive("g_left%d" % second, quarter(right_j, second))
        send("g_on_left%d" % part, quarter(right_j, second), quarter(right_j, second), to_left)
        receive("g_right%d" % second, quarter(left_j, second))
        send("m_left%d" % part, half(left_j, part), half(left_j, part), mate)
        receive("g_left%d" % first, quarter(right_j, first))
        send("m_right%d" % part, half(right_j, part), half(right_j, part), mate)

    def from_y(name, line):
        for offset in range(NZ):
            origin = (z + offset) % NZ
            receive(
                name + str(offset),
                wo.at[
                    pl.ds(aligned(2 * line + origin // share, 256), 256),
                    pl.ds(aligned(origin % share, 128), 128),
                ],
            )

    from_y("wy_up", down)
    block = wo.at[pl.ds(aligned(2 * down, 256), 256), :]
    send("wy_on_up", block, block, at(yy=up))
    from_y("wy_down", up)
    block = wo.at[pl.ds(aligned(2 * up + 1, 256), 256), :]
    send("wy_on_down", block, block, at(yy=down))

    relay_x(0)

    relay_x(1)

    def product(index):
        return dot(gated[index], wo[pl.ds(aligned(index, 256), 256), :])

    for copy in sent[:early]:
        copy.wait_send()

    @pl.when(c == holder)
    def _():
        for copy in emb_copies():
            copy.wait_send()
        for _, copy in emb_relays():
            copy.wait_send()

    @pl.when(moves)
    def _():
        swap_copy().wait_send()

    receive("wy_on_up", wo.at[pl.ds(aligned(2 * opposite, 256), 256), :])
    receive("wy_on_down", wo.at[pl.ds(aligned(2 * opposite + 1, 256), 256), :])
    total[...] = product(j)
    total[...] += product(left_j)
    for part in range(2):
        receive("g_on_right%d" % part, quarter(across_j, 2 * part))
        receive("g_on_left%d" % part, quarter(across_j, 2 * part + 1))
        send("m_across%d" % part, half(across_j, part), half(across_j, part), mate)
        if part == 0:
            total[...] += product(right_j)
    receive("g_mate0", half(mate_j, 0))
    receive("g_mate1", half(mate_j, 1))
    total[...] += product(mate_j)
    for name, place in (("left", left), ("right", right), ("across", across)):
        index = place * NC + 1 - c
        if name == "across":
            total[...] += product(across_j)
        receive("m_" + name + "0", half(index, 0))
        receive("m_" + name + "1", half(index, 1))
        if name == "across":
            out_ref[...] = (total[...] + product(index)).astype(bf16)
        else:
            total[...] += product(index)

    for copy in sent[early:]:
        copy.wait_send()


SEMAPHORES = 240


def body(
    tokens,
    embedding,
    norm_gain,
    in_weight,
    short_taps,
    decay_rates,
    residue,
    skip_weight,
    out_weight,
):
    whole = pl.BlockSpec(memory_space=pltpu.VMEM)
    outside = pl.BlockSpec(memory_space=pl.ANY)
    vm = pltpu.VMEM
    return pl.pallas_call(
        kernel,
        out_shape=jax.ShapeDtypeStruct((512, 512), bf16),
        in_specs=[outside] * 9,
        out_specs=whole,
        scratch_shapes=[
            vm((4, 128), jnp.int32),
            vm((32, 128), f32),
            vm((1, 256), f32),
            vm((3, 7, 256), f32),
            vm((16, 16), f32),
            vm((16, 16), f32),
            vm((3, 128, 256), bf16),
            vm((512, 512), bf16),
            vm((3, 256, 128), bf16),
            vm((NY, 3, 64, 128), bf16),
            vm((NX, 512, 128), bf16),
            vm((512, 512), bf16),
            vm((NX * NC, 1, 512), f32),
            vm((NZ, 16, 512), bf16),
            vm((NZ, 16, 256), bf16),
            vm((NZ, 16, 512), bf16),
            vm((NZ, 16, 256), bf16),
            vm((16, 512), f32),
            vm((16, 256), f32),
            vm((24, 512), f32),
            vm((NY, NZ, 4, 128), jnp.int32),
            vm((128, 128), f32),
            vm((128, 128), f32),
            vm((64, 128, 256), bf16),
            vm((3, 1088, 128), f32),
            vm((3, 7, 8, 128), f32),
            vm((1024, 128), f32),
            vm((1024, 128), f32),
            vm((128, 1024), f32),
            vm((1024, 128), f32),
            vm((1024, 128), bf16),
            vm((NY * NZ, 32, 128), bf16),
            vm((NX * NC, 512, 256), bf16),
            vm((2048, 512), bf16),
            vm((512, 512), f32),
            pltpu.SemaphoreType.DMA((8,)),
            pltpu.SemaphoreType.DMA((SEMAPHORES,)),
            pltpu.SemaphoreType.DMA((SEMAPHORES,)),
        ],
        compiler_params=pltpu.CompilerParams(
            collective_id=0, has_side_effects=True, vmem_limit_bytes=60 * 1024 * 1024
        ),
    )(
        tokens.reshape(4, 128),
        norm_gain.reshape(32, 128),
        skip_weight.reshape(1, 256),
        short_taps.transpose(1, 0, 2),
        decay_rates,
        residue,
        in_weight.transpose(1, 0, 2),
        embedding,
        out_weight,
    )


def solution(mesh):
    placed = (
        P("ctx"),
        P(None, "fsdp"),
        P(),
        P("ctx", None, "fsdp"),
        P(None, None, "fsdp"),
        P(None, "fsdp"),
        P(None, "fsdp"),
        P("fsdp"),
        P("fsdp", "ctx"),
    )
    return jax.shard_map(
        body, mesh=mesh, in_specs=placed, out_specs=P("ctx", "fsdp"), check_vma=False
    )
```

```python
import functools

import jax
import jax.numpy as jnp
from jax import lax
from jax.experimental import pallas as pl
from jax.experimental.pallas import tpu as pltpu
from jax.sharding import PartitionSpec as P

GROUP = 16
CHUNK = 128
NY, NZ, NX, NC = 4, 8, 4, 2
f32 = jnp.float32
bf16 = jnp.bfloat16
MESH = pl.DeviceIdType.MESH


def split(value):
    high = value.astype(bf16)
    return high, (value - high.astype(f32)).astype(bf16)


def dot(a, b):
    return jnp.dot(a, b, preferred_element_type=f32)


def dot_three(a, b):
    a_high, a_low = split(a)
    b_high, b_low = split(b)
    return dot(a_high, b_high) + dot(a_low, b_high) + dot(a_high, b_low)


def dot_nt(a, b):
    return lax.dot_general(a, b, (((1,), (1,)), ((), ())), preferred_element_type=f32)


def aligned(index, size):
    return pl.multiple_of(index * size, size)


def kernel(
    tokens_in,
    gain_in,
    skip_in,
    taps_in,
    rates_in,
    residue_in,
    w_in,
    emb_in,
    ow_ref,
    out_ref,
    tokens_ref,
    gain_ref,
    skip_ref,
    taps_ref,
    rates_ref,
    residue_ref,
    w_ref,
    emb_ref,
    wt,
    wbuf,
    ebuf,
    enorm,
    squares,
    send_kv,
    send_q,
    arrived_kv,
    arrived_q,
    own_kv,
    own_q,
    table,
    tokens,
    token_mat,
    token_page,
    one_hot,
    short_in,
    taps,
    driving,
    queries,
    convolved,
    gated_f,
    gated_b,
    landed,
    gated,
    wo,
    total,
    load_sems,
    send_sems,
    recv_sems,
):
    i = lax.axis_index("ctx")
    j = lax.axis_index("fsdp")
    y, z = i // NZ, i % NZ
    x, c = j // NC, j % NC
    up, down = (y + 1) % NY, (y + NY - 1) % NY
    opposite = (y + 2) % NY
    right, left = (x + 1) % NX, (x + NX - 1) % NX
    across = (x + 2) % NX
    count_ctx = NY * NZ
    count_fsdp = NX * NC
    share = count_ctx // count_fsdp

    def at(yy=None, zz=None, xx=None, cc=None):
        yy = y if yy is None else yy
        zz = z if zz is None else zz
        xx = x if xx is None else xx
        cc = c if cc is None else cc
        return (yy * NZ + zz, xx * NC + cc)

    labels = {}
    sent = []

    def slot(name):
        return labels.setdefault(name, len(labels))

    def remote(name, source, target, device):
        k = slot(name)
        return pltpu.make_async_remote_copy(
            src_ref=source,
            dst_ref=target,
            send_sem=send_sems.at[k],
            recv_sem=recv_sems.at[k],
            device_id=device,
            device_id_type=MESH,
        )

    def send(name, source, target, device):
        copy = remote(name, source, target, device)
        copy.start()
        sent.append(copy)

    def receive(name, target):
        pltpu.make_async_copy(target, target, recv_sems.at[slot(name)]).wait()

    def load(k, source, target):
        copy = pltpu.make_async_copy(source, target, load_sems.at[k])
        copy.start()
        return copy

    emb_load = load(0, emb_in, emb_ref)
    w_load = load(1, w_in, w_ref)
    small_loads = [
        load(2, tokens_in, tokens_ref),
        load(3, gain_in, gain_ref),
        load(4, skip_in, skip_ref),
        load(5, taps_in, taps_ref),
        load(6, rates_in, rates_ref),
        load(7, residue_in, residue_ref),
    ]

    barrier = pltpu.get_barrier_semaphore()

    def greet(device):
        pl.semaphore_signal(barrier, inc=1, device_id=device, device_id_type=MESH)

    for d in range(1, NZ):
        greet(at(zz=(z + d) % NZ))
    for d in range(1, NY):
        greet(at(yy=(y + d) % NY))
    for d in range(1, count_fsdp):
        greet((i, (j + d) % count_fsdp))
    swap_to = (share * j + i % share, i // share)
    moves = jnp.logical_or(swap_to[0] != i, swap_to[1] != j)

    @pl.when(moves)
    def _():
        greet(swap_to)

    w_load.wait()
    for group in range(3):
        for h in range(2):
            block = w_ref[group, :, h * 128 : (h + 1) * 128].astype(f32)
            wt[group, h * 128 : (h + 1) * 128, :] = block.T.astype(bf16)
    for copy in small_loads:
        copy.wait()
    pl.semaphore_wait(barrier, NZ - 1 + NY - 1 + count_fsdp - 1 + jnp.where(moves, 1, 0))

    wo_rows = pl.ds(aligned(2 * y + z // share, 256), 256)
    wo_cols = pl.ds(aligned(z % share, 128), 128)
    wo_own = wo.at[wo_rows, wo_cols]

    def swap_copy():
        return remote("swap", ow_ref, wo.at[pl.ds(aligned(j, 256), 256), wo_cols], swap_to)

    @pl.when(moves)
    def _():
        swap_copy().start()

    @pl.when(jnp.logical_not(moves))
    def _():
        pltpu.make_async_copy(ow_ref, wo_own, recv_sems.at[slot("swap")]).start()

    emb_load.wait()
    holder = z // share
    e_slots = [slot("e" + str(k)) for k in range(NX)]
    emb_piece = emb_ref.at[:, pl.ds(aligned(z % share, 128), 128)]

    def emb_copy(k, source, place, device):
        return pltpu.make_async_remote_copy(
            src_ref=source,
            dst_ref=ebuf.at[place],
            send_sem=send_sems.at[slot("es" + str(k))],
            recv_sem=recv_sems.at[e_slots[0] + place],
            device_id=device,
            device_id_type=MESH,
        )

    mate = at(cc=1 - c)

    def emb_copies():
        copies = [emb_copy(d, emb_piece, x, at(xx=(x + d) % NX)) for d in (2, 1, 3)]
        return copies + [emb_copy(0, emb_piece, x, mate)]

    def emb_relays():
        places = [(x + d) % NX for d in (1, 3, 2)]
        return [(place, emb_copy(4 + n, ebuf.at[place], place, mate)) for n, place in enumerate(places)]

    @pl.when(c == holder)
    def _():
        for copy in emb_copies():
            copy.start()
        pltpu.make_async_copy(emb_piece, ebuf.at[x], recv_sems.at[e_slots[0] + x]).start()

    def w_rows(to):
        return wt.at[:, pl.ds(aligned(to, 64), 64), :]

    for d in (2, 1, 3):
        to = (y + d) % NY
        send("w" + str(d), w_rows(to), wbuf.at[y], at(yy=to))

    for d in range(1, NZ):
        send("tz" + str(d), tokens_ref, tokens.at[y, z], at(zz=(z + d) % NZ))
    wbuf[y] = wt[:, pl.ds(aligned(y, 64), 64), :]
    tokens[y, z] = tokens_ref[...]

    ones = jnp.ones((8, 512), bf16)
    piece = emb_ref[...].astype(f32)
    high, low = split(piece * piece)
    squares[j] = (dot_nt(ones, high) + dot_nt(ones, low))[0:1, :]

    for d in range(1, count_fsdp):
        send("sq" + str(d), squares.at[j], squares.at[j], (i, (j + d) % count_fsdp))

    row = lax.broadcasted_iota(jnp.int32, (CHUNK, CHUNK), 0)
    lane = lax.broadcasted_iota(jnp.int32, (CHUNK, CHUNK), 1)
    group_lane = lax.broadcasted_iota(jnp.int32, (16, 16), 1) == i // 2
    rate = jnp.sum(jnp.where(group_lane, rates_ref[...], 0.0), axis=1, keepdims=True)
    weight = jnp.sum(jnp.where(group_lane, residue_ref[...], 0.0), axis=1, keepdims=True)
    steps = lax.broadcasted_iota(jnp.int32, (16, CHUNK), 1).astype(f32)
    rate = jnp.broadcast_to(rate, (16, CHUNK))
    weight = jnp.broadcast_to(weight, (16, CHUNK))
    filters = jnp.sum(weight * jnp.exp(-rate * steps), axis=0, keepdims=True)
    rolled = pltpu.roll(jnp.broadcast_to(filters, (CHUNK, CHUNK)), 0, 1, stride=1, stride_axis=0)
    toeplitz = jnp.where(lane >= row, rolled, 0.0).T
    to_end = jnp.exp(-rate * (CHUNK - 1 - steps))
    from_start = weight * jnp.exp(-rate * (steps + 1.0))
    from_start = jnp.concatenate([from_start, jnp.zeros((CHUNK - 16, CHUNK), f32)], axis=0).T

    pick = lax.broadcasted_iota(jnp.int32, (8, 256), 1) == 8 * i + lax.broadcasted_iota(jnp.int32, (8, 256), 0)
    skips = jnp.sum(jnp.where(pick, skip_ref[...], 0.0), axis=1, keepdims=True)
    skips = jnp.broadcast_to(skips, (8, CHUNK))
    for group in range(3):
        for lag in range(7):
            value = jnp.where(pick, taps_ref[group, lag : lag + 1, :], 0.0)
            taps[group, lag] = jnp.broadcast_to(jnp.sum(value, axis=1, keepdims=True), (8, CHUNK))

    receive("swap", wo_own)
    for d in (2, 6, 1, 7):
        send("wz" + str(d), wo_own, wo_own, at(zz=(z + d) % NZ))

    @pl.when(c == holder)
    def _():
        pltpu.make_async_copy(ebuf.at[x], ebuf.at[x], recv_sems.at[e_slots[0] + x]).wait()
        for place, copy in emb_relays():
            pltpu.make_async_copy(ebuf.at[place], ebuf.at[place], recv_sems.at[e_slots[0] + place]).wait()
            copy.start()

    @pl.when(c != holder)
    def _():
        for k in range(NX):
            pltpu.make_async_copy(ebuf.at[k], ebuf.at[k], recv_sems.at[e_slots[k]]).wait()

    for k in range(NY):
        gain = gain_ref[pl.ds(k * NZ + z, 1), :]
        enorm[:, k * 128 : (k + 1) * 128] = (ebuf[k].astype(f32) * gain).astype(bf16)
    for d in range(1, NY):
        receive("w" + str(d), wbuf.at[(y + NY - d) % NY])

    def partial(group):
        weights = jnp.concatenate([wbuf[k, group] for k in range(NY)], axis=1)
        return dot_nt(weights, enorm[...])

    keys, values = partial(1), partial(2)
    for k in range(NZ):
        part = slice(k * 8, (k + 1) * 8)
        send_kv[k] = jnp.concatenate([keys[part], values[part]], axis=0).astype(bf16)
    for d in (4, 3, 5, 2, 6, 1, 7):
        to = (z + d) % NZ
        send("kv" + str(d), send_kv.at[to], arrived_kv.at[z], at(zz=to))
    asks = partial(0)
    for k in range(NZ):
        part = slice(k * 8, (k + 1) * 8)
        send_q[k] = jnp.concatenate([asks[part, 0:256], asks[part, 256:512]], axis=0).astype(bf16)
    for d in (4, 3, 5, 2, 6, 1, 7):
        to = (z + d) % NZ
        send("q" + str(d), send_q.at[to], arrived_q.at[z], at(zz=to))
    own_kv[...] = send_kv[z].astype(f32)
    own_q[...] = send_q[z].astype(f32)

    for d in range(1, NZ):
        receive("tz" + str(d), tokens.at[y, (z + NZ - d) % NZ])
    for d in range(1, NY):
        send("ty" + str(d), tokens.at[y], tokens.at[y], at(yy=(y + d) % NY))

    for d in range(1, NY):
        receive("ty" + str(d), tokens.at[(y + NY - d) % NY])
    for k in range(count_ctx):
        these = tokens[k // NZ, k % NZ]
        token_mat[k * 4 : (k + 1) * 4, :] = (these % 128).astype(f32)
        token_page[k * 4 : (k + 1) * 4, :] = (these // 128).astype(f32)
    token_mat[...] = token_mat[...].T
    token_page[...] = token_page[...].T
    def wo_place(origin, half=None):
        rows, first = (256, 0) if half is None else (128, half * 128)
        return wo.at[
            pl.ds(aligned(2 * y + origin // share, 256) + first, rows),
            pl.ds(aligned(origin % share, 128), 128),
        ]

    for d in (1, 7, 2, 6):
        receive("wz" + str(d), wo_place((z + NZ - d) % NZ))
    def along_y(offset):
        block = wo_place((z + offset) % NZ)
        send("wy_up%d" % offset, block, block, at(yy=up))
        send("wy_down%d" % offset, block, block, at(yy=down))

    for offset in (0, 1, 7, 2, 6):
        along_y(offset)

    vocab_row = row.astype(f32)

    def mark(n, carry):
        for h in range(2):
            these = token_mat[pl.ds(2 * n + h, 1), :]
            hits = jnp.where(vocab_row == these, 1.0, 0.0)
            one_hot[n, :, h * 128 : (h + 1) * 128] = hits.astype(bf16)
        return carry

    lax.fori_loop(0, 64, mark, 0, unroll=2)

    for d in range(1, count_fsdp):
        receive("sq" + str(d), squares.at[(j + count_fsdp - d) % count_fsdp])
    all_squares = squares[0]
    for k in range(1, count_fsdp):
        all_squares = all_squares + squares[k]
    width = gain_ref.shape[0] * gain_ref.shape[1]
    scale = lax.rsqrt(all_squares * (1.0 / width) + 1e-05)

    value = own_kv[...]
    for d in (1, 7, 2, 6, 3, 5, 4):
        origin = (z + NZ - d) % NZ
        receive("kv" + str(d), arrived_kv.at[origin])
        value = value + arrived_kv[origin].astype(f32)
    table[8:24, :] = value * scale
    value = own_q[...]
    for d in (1, 7, 2, 6, 3, 5, 4):
        origin = (z + NZ - d) % NZ
        receive("q" + str(d), arrived_q.at[origin])
        value = value + arrived_q[origin].astype(f32)
    table[0:8, :] = jnp.concatenate([value[0:8], value[8:16]], axis=1) * scale

    ahead, behind = at(zz=(z + 2) % NZ), at(zz=(z + NZ - 2) % NZ)
    block = wo_place((z + NZ - 1) % NZ)
    send("wz3", block, block, ahead)
    block = wo_place((z + 1) % NZ)
    send("wz5", block, block, behind)
    block = wo_place((z + NZ - 2) % NZ, 0)
    send("wz4a", block, block, ahead)
    block = wo_place((z + 2) % NZ, 1)
    send("wz4b", block, block, behind)

    pages = [table[0:24, k * 128 : (k + 1) * 128] for k in range(4)]
    table16 = jnp.concatenate(pages, axis=0).astype(bf16)

    def look_up(n, carry):
        found = dot(table16, one_hot[n])
        for h in range(2):
            page = jnp.broadcast_to(token_page[pl.ds(2 * n + h, 1), :], (24, 128))
            options = [found[k * 24 : (k + 1) * 24, h * 128 : (h + 1) * 128] for k in range(4)]
            low = jnp.where(page == 0.0, options[0], options[1])
            high = jnp.where(page == 2.0, options[2], options[3])
            value = jnp.where(page < 2.0, low, high)
            rows = pl.ds(aligned(2 * n + h + 8, 8), 8)
            for group in range(3):
                short_in[group, rows, :] = value[group * 8 : (group + 1) * 8]
        return carry

    lax.fori_loop(0, 64, look_up, 0, unroll=16)
    for group in range(3):
        tail = short_in[group, 1024:1088, :]
        shifted = pltpu.roll(tail, 1, 1)
        first_lane = lax.broadcasted_iota(jnp.int32, (64, 128), 1) == 0
        short_in[group, 0:64, :] = jnp.where(first_lane, 0.0, shifted)

    def convolve(n, carry):
        sums = []
        for group in range(3):
            result = taps[group, 0] * short_in[group, pl.ds(aligned(n + 8, 8), 8), :]
            for lag in range(1, 7):
                rows = pl.ds(aligned(n + 8 - lag, 8), 8)
                result = result + taps[group, lag] * short_in[group, rows, :]
            sums.append(result)
        here = pl.ds(aligned(n, 8), 8)
        queries[here, :] = sums[0]
        driving[here, :] = sums[1] * sums[2]
        return carry

    lax.fori_loop(0, 128, convolve, 0, unroll=16)

    planes = [driving[pl.ds(k, CHUNK, stride=8), :] for k in range(8)]
    wide = jnp.concatenate(planes, axis=1)
    ends = dot_three(to_end, wide)
    states = jnp.concatenate([ends[:, k * 128 : (k + 1) * 128] for k in range(8)], axis=0)
    rates = jnp.concatenate([rate] * 8, axis=0)

    def later(value, count):
        return jnp.where(lane >= count, pltpu.roll(value, count, 1), 0.0)

    for level in range(7):
        reach = 1 << level
        states = states + jnp.exp(-rates * float(CHUNK * reach)) * later(states, reach)
    states = later(states, 1)
    starts = jnp.concatenate([states[k * 16 : (k + 1) * 16] for k in range(8)], axis=1)
    starts = jnp.concatenate([starts, jnp.zeros((CHUNK - 16, 1024), f32)], axis=0)
    convolved[...] = dot_three(toeplitz, wide) + dot_three(from_start, starts)
    for k in range(8):
        response = convolved[:, k * 128 : (k + 1) * 128] + skips[k : k + 1, :] * planes[k]
        result = queries[pl.ds(k, CHUNK, stride=8), :] * response
        gated_f[pl.ds(k, CHUNK, stride=8), :] = result.T
    gated_b[...] = gated_f[...].astype(bf16)

    far = sorted(range(1, count_ctx), key=lambda d: -min(d % NZ, NZ - d % NZ))
    for part in range(2):
        for d in far:
            to = (i + d) % count_ctx
            rows = pl.ds(aligned(2 * to + part, 16), 16)
            send("a%d_%d" % (part, d), gated_b.at[rows, :], landed.at[i, pl.ds(16 * part, 16), :], (to, j))
    receive("wz3", wo_place((z + NZ - 3) % NZ))
    receive("wz5", wo_place((z + 3) % NZ))
    receive("wz4a", wo_place((z + 4) % NZ, 0))
    receive("wz4b", wo_place((z + 4) % NZ, 1))
    for offset in (3, 5, 4):
        along_y(offset)

    landed[i] = gated_b[pl.ds(aligned(i, 32), 32), :]

    left_j, right_j, across_j = left * NC + c, right * NC + c, across * NC + c
    mate_j = x * NC + 1 - c
    to_right, to_left = at(xx=right), at(xx=left)

    def quarter(index, k):
        return gated.at[index, pl.ds(128 * k, 128), :]

    def half(index, part):
        return gated.at[index, pl.ds(256 * part, 256), :]

    early = len(sent)
    for part in range(2):
        for d in reversed(far):
            origin = (i + count_ctx - d) % count_ctx
            receive("a%d_%d" % (part, d), landed.at[origin, pl.ds(16 * part, 16), :])
        blocks = [landed[n, part * 16 : part * 16 + 16, :].astype(f32) for n in range(count_ctx)]
        for k in range(2):
            for h in range(2):
                block = [blocks[n][k * 8 : (k + 1) * 8] for n in range(h * 16, (h + 1) * 16)]
                block = jnp.concatenate(block, axis=0)
                rows = slice((2 * part + k) * 128, (2 * part + k + 1) * 128)
                gated[j, rows, h * 128 : (h + 1) * 128] = block.T.astype(bf16)
        first, second = 2 * part, 2 * part + 1
        send("g_right%d" % first, quarter(j, first), quarter(j, first), to_right)
        send("g_left%d" % second, quarter(j, second), quarter(j, second), to_left)
        send("g_right%d" % second, quarter(j, second), quarter(j, second), to_right)
        send("g_left%d" % first, quarter(j, first), quarter(j, first), to_left)
        send("g_mate%d" % part, half(j, part), half(j, part), mate)

    def relay_x(part):
        first, second = 2 * part, 2 * part + 1
        receive("g_right%d" % first, quarter(left_j, first))
        send("g_on_right%d" % part, quarter(left_j, first), quarter(left_j, first), to_right)
        receive("g_left%d" % second, quarter(right_j, second))
        send("g_on_left%d" % part, quarter(right_j, second), quarter(right_j, second), to_left)
        receive("g_right%d" % second, quarter(left_j, second))
        send("m_left%d" % part, half(left_j, part), half(left_j, part), mate)
        receive("g_left%d" % first, quarter(right_j, first))
        send("m_right%d" % part, half(right_j, part), half(right_j, part), mate)

    def from_y(name, line):
        for offset in range(NZ):
            origin = (z + offset) % NZ
            receive(
                name + str(offset),
                wo.at[
                    pl.ds(aligned(2 * line + origin // share, 256), 256),
                    pl.ds(aligned(origin % share, 128), 128),
                ],
            )

    from_y("wy_up", down)
    block = wo.at[pl.ds(aligned(2 * down, 256), 256), :]
    send("wy_on_up", block, block, at(yy=up))
    from_y("wy_down", up)
    block = wo.at[pl.ds(aligned(2 * up + 1, 256), 256), :]
    send("wy_on_down", block, block, at(yy=down))

    relay_x(0)

    relay_x(1)

    def product(index):
        return dot(gated[index], wo[pl.ds(aligned(index, 256), 256), :])

    for copy in sent[:early]:
        copy.wait_send()

    @pl.when(c == holder)
    def _():
        for copy in emb_copies():
            copy.wait_send()
        for _, copy in emb_relays():
            copy.wait_send()

    @pl.when(moves)
    def _():
        swap_copy().wait_send()

    receive("wy_on_up", wo.at[pl.ds(aligned(2 * opposite, 256), 256), :])
    receive("wy_on_down", wo.at[pl.ds(aligned(2 * opposite + 1, 256), 256), :])
    total[...] = product(j)
    total[...] += product(left_j)
    for part in range(2):
        receive("g_on_right%d" % part, quarter(across_j, 2 * part))
        receive("g_on_left%d" % part, quarter(across_j, 2 * part + 1))
        send("m_across%d" % part, half(across_j, part), half(across_j, part), mate)
        if part == 0:
            total[...] += product(right_j)
    receive("g_mate0", half(mate_j, 0))
    receive("g_mate1", half(mate_j, 1))
    total[...] += product(mate_j)
    for name, place in (("left", left), ("right", right), ("across", across)):
        index = place * NC + 1 - c
        if name == "across":
            total[...] += product(across_j)
        receive("m_" + name + "0", half(index, 0))
        receive("m_" + name + "1", half(index, 1))
        if name == "across":
            out_ref[...] = (total[...] + product(index)).astype(bf16)
        else:
            total[...] += product(index)

    for copy in sent[early:]:
        copy.wait_send()


SEMAPHORES = 240


def body(
    tokens,
    embedding,
    norm_gain,
    in_weight,
    short_taps,
    decay_rates,
    residue,
    skip_weight,
    out_weight,
):
    whole = pl.BlockSpec(memory_space=pltpu.VMEM)
    outside = pl.BlockSpec(memory_space=pl.ANY)
    vm = pltpu.VMEM
    return pl.pallas_call(
        kernel,
        out_shape=jax.ShapeDtypeStruct((512, 512), bf16),
        in_specs=[outside] * 9,
        out_specs=whole,
        scratch_shapes=[
            vm((4, 128), jnp.int32),
            vm((32, 128), f32),
            vm((1, 256), f32),
            vm((3, 7, 256), f32),
            vm((16, 16), f32),
            vm((16, 16), f32),
            vm((3, 128, 256), bf16),
            vm((512, 512), bf16),
            vm((3, 256, 128), bf16),
            vm((NY, 3, 64, 128), bf16),
            vm((NX, 512, 128), bf16),
            vm((512, 512), bf16),
            vm((NX * NC, 1, 512), f32),
            vm((NZ, 16, 512), bf16),
            vm((NZ, 16, 256), bf16),
            vm((NZ, 16, 512), bf16),
            vm((NZ, 16, 256), bf16),
            vm((16, 512), f32),
            vm((16, 256), f32),
            vm((24, 512), f32),
            vm((NY, NZ, 4, 128), jnp.int32),
            vm((128, 128), f32),
            vm((128, 128), f32),
            vm((64, 128, 256), bf16),
            vm((3, 1088, 128), f32),
            vm((3, 7, 8, 128), f32),
            vm((1024, 128), f32),
            vm((1024, 128), f32),
            vm((128, 1024), f32),
            vm((1024, 128), f32),
            vm((1024, 128), bf16),
            vm((NY * NZ, 32, 128), bf16),
            vm((NX * NC, 512, 256), bf16),
            vm((2048, 512), bf16),
            vm((512, 512), f32),
            pltpu.SemaphoreType.DMA((8,)),
            pltpu.SemaphoreType.DMA((SEMAPHORES,)),
            pltpu.SemaphoreType.DMA((SEMAPHORES,)),
        ],
        compiler_params=pltpu.CompilerParams(
            collective_id=0, has_side_effects=True, vmem_limit_bytes=60 * 1024 * 1024
        ),
    )(
        tokens.reshape(4, 128),
        norm_gain.reshape(32, 128),
        skip_weight.reshape(1, 256),
        short_taps.transpose(1, 0, 2),
        decay_rates,
        residue,
        in_weight.transpose(1, 0, 2),
        embedding,
        out_weight,
    )


def solution(mesh):
    placed = (
        P("ctx"),
        P(None, "fsdp"),
        P(),
        P("ctx", None, "fsdp"),
        P(None, None, "fsdp"),
        P(None, "fsdp"),
        P(None, "fsdp"),
        P("fsdp"),
        P("fsdp", "ctx"),
    )
    return jax.shard_map(
        body, mesh=mesh, in_specs=placed, out_specs=P("ctx", "fsdp"), check_vma=False
    )
```

```python
import functools

import jax
import jax.numpy as jnp
from jax import lax
from jax.experimental import pallas as pl
from jax.experimental.pallas import tpu as pltpu
from jax.sharding import PartitionSpec as P

GROUP = 16
CHUNK = 128
NY, NZ, NX, NC = 4, 8, 4, 2
f32 = jnp.float32
bf16 = jnp.bfloat16
MESH = pl.DeviceIdType.MESH


def split(value):
    high = value.astype(bf16)
    return high, (value - high.astype(f32)).astype(bf16)


def dot(a, b):
    return jnp.dot(a, b, preferred_element_type=f32)


def dot_three(a, b):
    a_high, a_low = split(a)
    b_high, b_low = split(b)
    return dot(a_high, b_high) + dot(a_low, b_high) + dot(a_high, b_low)


def dot_nt(a, b):
    return lax.dot_general(a, b, (((1,), (1,)), ((), ())), preferred_element_type=f32)


def aligned(index, size):
    return pl.multiple_of(index * size, size)


def kernel(
    tokens_in,
    gain_in,
    skip_in,
    taps_in,
    rates_in,
    residue_in,
    w_in,
    emb_in,
    ow_ref,
    out_ref,
    tokens_ref,
    gain_ref,
    skip_ref,
    taps_ref,
    rates_ref,
    residue_ref,
    w_ref,
    emb_ref,
    wt,
    wbuf,
    ebuf,
    enorm,
    squares,
    send_kv,
    send_q,
    arrived_kv,
    arrived_q,
    own_kv,
    own_q,
    table,
    tokens,
    token_mat,
    token_page,
    one_hot,
    short_in,
    taps,
    driving,
    queries,
    convolved,
    gated_f,
    gated_b,
    landed,
    gated,
    wo,
    total,
    load_sems,
    send_sems,
    recv_sems,
):
    i = lax.axis_index("ctx")
    j = lax.axis_index("fsdp")
    y, z = i // NZ, i % NZ
    x, c = j // NC, j % NC
    up, down = (y + 1) % NY, (y + NY - 1) % NY
    opposite = (y + 2) % NY
    right, left = (x + 1) % NX, (x + NX - 1) % NX
    across = (x + 2) % NX
    count_ctx = NY * NZ
    count_fsdp = NX * NC
    share = count_ctx // count_fsdp

    def at(yy=None, zz=None, xx=None, cc=None):
        yy = y if yy is None else yy
        zz = z if zz is None else zz
        xx = x if xx is None else xx
        cc = c if cc is None else cc
        return (yy * NZ + zz, xx * NC + cc)

    labels = {}
    sent = []

    def slot(name):
        return labels.setdefault(name, len(labels))

    def remote(name, source, target, device):
        k = slot(name)
        return pltpu.make_async_remote_copy(
            src_ref=source,
            dst_ref=target,
            send_sem=send_sems.at[k],
            recv_sem=recv_sems.at[k],
            device_id=device,
            device_id_type=MESH,
        )

    def send(name, source, target, device):
        copy = remote(name, source, target, device)
        copy.start()
        sent.append(copy)

    def receive(name, target):
        pltpu.make_async_copy(target, target, recv_sems.at[slot(name)]).wait()

    def load(k, source, target):
        copy = pltpu.make_async_copy(source, target, load_sems.at[k])
        copy.start()
        return copy

    emb_load = load(0, emb_in, emb_ref)
    w_load = load(1, w_in, w_ref)
    small_loads = [
        load(2, tokens_in, tokens_ref),
        load(3, gain_in, gain_ref),
        load(4, skip_in, skip_ref),
        load(5, taps_in, taps_ref),
        load(6, rates_in, rates_ref),
        load(7, residue_in, residue_ref),
    ]

    barrier = pltpu.get_barrier_semaphore()

    def greet(device):
        pl.semaphore_signal(barrier, inc=1, device_id=device, device_id_type=MESH)

    for d in range(1, NZ):
        greet(at(zz=(z + d) % NZ))
    for d in range(1, NY):
        greet(at(yy=(y + d) % NY))
    for d in range(1, count_fsdp):
        greet((i, (j + d) % count_fsdp))
    swap_to = (share * j + i % share, i // share)
    moves = jnp.logical_or(swap_to[0] != i, swap_to[1] != j)

    @pl.when(moves)
    def _():
        greet(swap_to)

    w_load.wait()
    for group in range(3):
        for h in range(2):
            block = w_ref[group, :, h * 128 : (h + 1) * 128].astype(f32)
            wt[group, h * 128 : (h + 1) * 128, :] = block.T.astype(bf16)
    for copy in small_loads:
        copy.wait()
    pl.semaphore_wait(barrier, NZ - 1 + NY - 1 + count_fsdp - 1 + jnp.where(moves, 1, 0))

    wo_rows = pl.ds(aligned(2 * y + z // share, 256), 256)
    wo_cols = pl.ds(aligned(z % share, 128), 128)
    wo_own = wo.at[wo_rows, wo_cols]

    def swap_copy():
        return remote("swap", ow_ref, wo.at[pl.ds(aligned(j, 256), 256), wo_cols], swap_to)

    @pl.when(moves)
    def _():
        swap_copy().start()

    @pl.when(jnp.logical_not(moves))
    def _():
        pltpu.make_async_copy(ow_ref, wo_own, recv_sems.at[slot("swap")]).start()

    emb_load.wait()
    holder = z // share
    e_slots = [slot("e" + str(k)) for k in range(NX)]
    emb_piece = emb_ref.at[:, pl.ds(aligned(z % share, 128), 128)]

    def emb_copy(k, source, place, device):
        return pltpu.make_async_remote_copy(
            src_ref=source,
            dst_ref=ebuf.at[place],
            send_sem=send_sems.at[slot("es" + str(k))],
            recv_sem=recv_sems.at[e_slots[0] + place],
            device_id=device,
            device_id_type=MESH,
        )

    mate = at(cc=1 - c)

    def emb_copies():
        copies = [emb_copy(d, emb_piece, x, at(xx=(x + d) % NX)) for d in (2, 1, 3)]
        return copies + [emb_copy(0, emb_piece, x, mate)]

    def emb_relays():
        places = [(x + d) % NX for d in (1, 3, 2)]
        return [(place, emb_copy(4 + n, ebuf.at[place], place, mate)) for n, place in enumerate(places)]

    @pl.when(c == holder)
    def _():
        for copy in emb_copies():
            copy.start()
        pltpu.make_async_copy(emb_piece, ebuf.at[x], recv_sems.at[e_slots[0] + x]).start()

    def w_rows(to):
        return wt.at[:, pl.ds(aligned(to, 64), 64), :]

    for d in (2, 1, 3):
        to = (y + d) % NY
        send("w" + str(d), w_rows(to), wbuf.at[y], at(yy=to))

    for d in range(1, NZ):
        send("tz" + str(d), tokens_ref, tokens.at[y, z], at(zz=(z + d) % NZ))
    wbuf[y] = wt[:, pl.ds(aligned(y, 64), 64), :]
    tokens[y, z] = tokens_ref[...]

    ones = jnp.ones((8, 512), bf16)
    piece = emb_ref[...].astype(f32)
    high, low = split(piece * piece)
    squares[j] = (dot_nt(ones, high) + dot_nt(ones, low))[0:1, :]

    for d in range(1, count_fsdp):
        send("sq" + str(d), squares.at[j], squares.at[j], (i, (j + d) % count_fsdp))

    row = lax.broadcasted_iota(jnp.int32, (CHUNK, CHUNK), 0)
    lane = lax.broadcasted_iota(jnp.int32, (CHUNK, CHUNK), 1)
    group_lane = lax.broadcasted_iota(jnp.int32, (16, 16), 1) == i // 2
    rate = jnp.sum(jnp.where(group_lane, rates_ref[...], 0.0), axis=1, keepdims=True)
    weight = jnp.sum(jnp.where(group_lane, residue_ref[...], 0.0), axis=1, keepdims=True)
    steps = lax.broadcasted_iota(jnp.int32, (16, CHUNK), 1).astype(f32)
    rate = jnp.broadcast_to(rate, (16, CHUNK))
    weight = jnp.broadcast_to(weight, (16, CHUNK))
    filters = jnp.sum(weight * jnp.exp(-rate * steps), axis=0, keepdims=True)
    rolled = pltpu.roll(jnp.broadcast_to(filters, (CHUNK, CHUNK)), 0, 1, stride=1, stride_axis=0)
    toeplitz = jnp.where(lane >= row, rolled, 0.0).T
    to_end = jnp.exp(-rate * (CHUNK - 1 - steps))
    from_start = weight * jnp.exp(-rate * (steps + 1.0))
    from_start = jnp.concatenate([from_start, jnp.zeros((CHUNK - 16, CHUNK), f32)], axis=0).T

    pick = lax.broadcasted_iota(jnp.int32, (8, 256), 1) == 8 * i + lax.broadcasted_iota(jnp.int32, (8, 256), 0)
    skips = jnp.sum(jnp.where(pick, skip_ref[...], 0.0), axis=1, keepdims=True)
    skips = jnp.broadcast_to(skips, (8, CHUNK))
    for group in range(3):
        for lag in range(7):
            value = jnp.where(pick, taps_ref[group, lag : lag + 1, :], 0.0)
            taps[group, lag] = jnp.broadcast_to(jnp.sum(value, axis=1, keepdims=True), (8, CHUNK))

    receive("swap", wo_own)
    for d in (2, 6, 1, 7):
        send("wz" + str(d), wo_own, wo_own, at(zz=(z + d) % NZ))

    @pl.when(c == holder)
    def _():
        pltpu.make_async_copy(ebuf.at[x], ebuf.at[x], recv_sems.at[e_slots[0] + x]).wait()
        for place, copy in emb_relays():
            pltpu.make_async_copy(ebuf.at[place], ebuf.at[place], recv_sems.at[e_slots[0] + place]).wait()
            copy.start()

    @pl.when(c != holder)
    def _():
        for k in range(NX):
            pltpu.make_async_copy(ebuf.at[k], ebuf.at[k], recv_sems.at[e_slots[k]]).wait()

    for k in range(NY):
        gain = gain_ref[pl.ds(k * NZ + z, 1), :]
        enorm[:, k * 128 : (k + 1) * 128] = (ebuf[k].astype(f32) * gain).astype(bf16)
    for d in range(1, NY):
        receive("w" + str(d), wbuf.at[(y + NY - d) % NY])

    def partial(group):
        weights = jnp.concatenate([wbuf[k, group] for k in range(NY)], axis=1)
        return dot_nt(weights, enorm[...])

    keys, values = partial(1), partial(2)
    for k in range(NZ):
        part = slice(k * 8, (k + 1) * 8)
        send_kv[k] = jnp.concatenate([keys[part], values[part]], axis=0).astype(bf16)
    for d in (4, 3, 5, 2, 6, 1, 7):
        to = (z + d) % NZ
        send("kv" + str(d), send_kv.at[to], arrived_kv.at[z], at(zz=to))
    asks = partial(0)
    for k in range(NZ):
        part = slice(k * 8, (k + 1) * 8)
        send_q[k] = jnp.concatenate([asks[part, 0:256], asks[part, 256:512]], axis=0).astype(bf16)
    for d in (4, 3, 5, 2, 6, 1, 7):
        to = (z + d) % NZ
        send("q" + str(d), send_q.at[to], arrived_q.at[z], at(zz=to))
    own_kv[...] = send_kv[z].astype(f32)
    own_q[...] = send_q[z].astype(f32)

    for d in range(1, NZ):
        receive("tz" + str(d), tokens.at[y, (z + NZ - d) % NZ])
    for d in range(1, NY):
        send("ty" + str(d), tokens.at[y], tokens.at[y], at(yy=(y + d) % NY))

    for d in range(1, NY):
        receive("ty" + str(d), tokens.at[(y + NY - d) % NY])
    for k in range(count_ctx):
        these = tokens[k // NZ, k % NZ]
        token_mat[k * 4 : (k + 1) * 4, :] = (these % 128).astype(f32)
        token_page[k * 4 : (k + 1) * 4, :] = (these // 128).astype(f32)
    token_mat[...] = token_mat[...].T
    token_page[...] = token_page[...].T
    def wo_place(origin, half=None):
        rows, first = (256, 0) if half is None else (128, half * 128)
        return wo.at[
            pl.ds(aligned(2 * y + origin // share, 256) + first, rows),
            pl.ds(aligned(origin % share, 128), 128),
        ]

    for d in (1, 7, 2, 6):
        receive("wz" + str(d), wo_place((z + NZ - d) % NZ))
    def along_y(offset):
        block = wo_place((z + offset) % NZ)
        send("wy_up%d" % offset, block, block, at(yy=up))
        send("wy_down%d" % offset, block, block, at(yy=down))

    for offset in (0, 1, 7, 2, 6):
        along_y(offset)

    vocab_row = row.astype(f32)

    def mark(n, carry):
        for h in range(2):
            these = token_mat[pl.ds(2 * n + h, 1), :]
            hits = jnp.where(vocab_row == these, 1.0, 0.0)
            one_hot[n, :, h * 128 : (h + 1) * 128] = hits.astype(bf16)
        return carry

    lax.fori_loop(0, 64, mark, 0, unroll=4)

    for d in range(1, count_fsdp):
        receive("sq" + str(d), squares.at[(j + count_fsdp - d) % count_fsdp])
    all_squares = squares[0]
    for k in range(1, count_fsdp):
        all_squares = all_squares + squares[k]
    width = gain_ref.shape[0] * gain_ref.shape[1]
    scale = lax.rsqrt(all_squares * (1.0 / width) + 1e-05)

    value = own_kv[...]
    for d in (1, 7, 2, 6, 3, 5, 4):
        origin = (z + NZ - d) % NZ
        receive("kv" + str(d), arrived_kv.at[origin])
        value = value + arrived_kv[origin].astype(f32)
    table[8:24, :] = value * scale
    value = own_q[...]
    for d in (1, 7, 2, 6, 3, 5, 4):
        origin = (z + NZ - d) % NZ
        receive("q" + str(d), arrived_q.at[origin])
        value = value + arrived_q[origin].astype(f32)
    table[0:8, :] = jnp.concatenate([value[0:8], value[8:16]], axis=1) * scale

    ahead, behind = at(zz=(z + 2) % NZ), at(zz=(z + NZ - 2) % NZ)
    block = wo_place((z + NZ - 1) % NZ)
    send("wz3", block, block, ahead)
    block = wo_place((z + 1) % NZ)
    send("wz5", block, block, behind)
    block = wo_place((z + NZ - 2) % NZ, 0)
    send("wz4a", block, block, ahead)
    block = wo_place((z + 2) % NZ, 1)
    send("wz4b", block, block, behind)

    pages = [table[0:24, k * 128 : (k + 1) * 128] for k in range(4)]
    table16 = jnp.concatenate(pages, axis=0).astype(bf16)

    def look_up(n, carry):
        found = dot(table16, one_hot[n])
        for h in range(2):
            page = jnp.broadcast_to(token_page[pl.ds(2 * n + h, 1), :], (24, 128))
            options = [found[k * 24 : (k + 1) * 24, h * 128 : (h + 1) * 128] for k in range(4)]
            low = jnp.where(page == 0.0, options[0], options[1])
            high = jnp.where(page == 2.0, options[2], options[3])
            value = jnp.where(page < 2.0, low, high)
            rows = pl.ds(aligned(2 * n + h + 8, 8), 8)
            for group in range(3):
                short_in[group, rows, :] = value[group * 8 : (group + 1) * 8]
        return carry

    lax.fori_loop(0, 64, look_up, 0, unroll=32)
    for group in range(3):
        tail = short_in[group, 1024:1088, :]
        shifted = pltpu.roll(tail, 1, 1)
        first_lane = lax.broadcasted_iota(jnp.int32, (64, 128), 1) == 0
        short_in[group, 0:64, :] = jnp.where(first_lane, 0.0, shifted)

    def convolve(n, carry):
        sums = []
        for group in range(3):
            result = taps[group, 0] * short_in[group, pl.ds(aligned(n + 8, 8), 8), :]
            for lag in range(1, 7):
                rows = pl.ds(aligned(n + 8 - lag, 8), 8)
                result = result + taps[group, lag] * short_in[group, rows, :]
            sums.append(result)
        here = pl.ds(aligned(n, 8), 8)
        queries[here, :] = sums[0]
        driving[here, :] = sums[1] * sums[2]
        return carry

    lax.fori_loop(0, 128, convolve, 0, unroll=32)

    planes = [driving[pl.ds(k, CHUNK, stride=8), :] for k in range(8)]
    wide = jnp.concatenate(planes, axis=1)
    ends = dot_three(to_end, wide)
    states = jnp.concatenate([ends[:, k * 128 : (k + 1) * 128] for k in range(8)], axis=0)
    rates = jnp.concatenate([rate] * 8, axis=0)

    def later(value, count):
        return jnp.where(lane >= count, pltpu.roll(value, count, 1), 0.0)

    for level in range(7):
        reach = 1 << level
        states = states + jnp.exp(-rates * float(CHUNK * reach)) * later(states, reach)
    states = later(states, 1)
    starts = jnp.concatenate([states[k * 16 : (k + 1) * 16] for k in range(8)], axis=1)
    starts = jnp.concatenate([starts, jnp.zeros((CHUNK - 16, 1024), f32)], axis=0)
    convolved[...] = dot_three(toeplitz, wide) + dot_three(from_start, starts)
    for k in range(8):
        response = convolved[:, k * 128 : (k + 1) * 128] + skips[k : k + 1, :] * planes[k]
        result = queries[pl.ds(k, CHUNK, stride=8), :] * response
        gated_f[pl.ds(k, CHUNK, stride=8), :] = result.T
    gated_b[...] = gated_f[...].astype(bf16)

    far = sorted(range(1, count_ctx), key=lambda d: -min(d % NZ, NZ - d % NZ))
    for part in range(2):
        for d in far:
            to = (i + d) % count_ctx
            rows = pl.ds(aligned(2 * to + part, 16), 16)
            send("a%d_%d" % (part, d), gated_b.at[rows, :], landed.at[i, pl.ds(16 * part, 16), :], (to, j))
    receive("wz3", wo_place((z + NZ - 3) % NZ))
    receive("wz5", wo_place((z + 3) % NZ))
    receive("wz4a", wo_place((z + 4) % NZ, 0))
    receive("wz4b", wo_place((z + 4) % NZ, 1))
    for offset in (3, 5, 4):
        along_y(offset)

    landed[i] = gated_b[pl.ds(aligned(i, 32), 32), :]

    left_j, right_j, across_j = left * NC + c, right * NC + c, across * NC + c
    mate_j = x * NC + 1 - c
    to_right, to_left = at(xx=right), at(xx=left)

    def quarter(index, k):
        return gated.at[index, pl.ds(128 * k, 128), :]

    def half(index, part):
        return gated.at[index, pl.ds(256 * part, 256), :]

    early = len(sent)
    for part in range(2):
        for d in reversed(far):
            origin = (i + count_ctx - d) % count_ctx
            receive("a%d_%d" % (part, d), landed.at[origin, pl.ds(16 * part, 16), :])
        blocks = [landed[n, part * 16 : part * 16 + 16, :].astype(f32) for n in range(count_ctx)]
        for k in range(2):
            for h in range(2):
                block = [blocks[n][k * 8 : (k + 1) * 8] for n in range(h * 16, (h + 1) * 16)]
                block = jnp.concatenate(block, axis=0)
                rows = slice((2 * part + k) * 128, (2 * part + k + 1) * 128)
                gated[j, rows, h * 128 : (h + 1) * 128] = block.T.astype(bf16)
        first, second = 2 * part, 2 * part + 1
        send("g_right%d" % first, quarter(j, first), quarter(j, first), to_right)
        send("g_left%d" % second, quarter(j, second), quarter(j, second), to_left)
        send("g_right%d" % second, quarter(j, second), quarter(j, second), to_right)
        send("g_left%d" % first, quarter(j, first), quarter(j, first), to_left)
        send("g_mate%d" % part, half(j, part), half(j, part), mate)

    def relay_x(part):
        first, second = 2 * part, 2 * part + 1
        receive("g_right%d" % first, quarter(left_j, first))
        send("g_on_right%d" % part, quarter(left_j, first), quarter(left_j, first), to_right)
        receive("g_left%d" % second, quarter(right_j, second))
        send("g_on_left%d" % part, quarter(right_j, second), quarter(right_j, second), to_left)
        receive("g_right%d" % second, quarter(left_j, second))
        send("m_left%d" % part, half(left_j, part), half(left_j, part), mate)
        receive("g_left%d" % first, quarter(right_j, first))
        send("m_right%d" % part, half(right_j, part), half(right_j, part), mate)

    def from_y(name, line):
        for offset in range(NZ):
            origin = (z + offset) % NZ
            receive(
                name + str(offset),
                wo.at[
                    pl.ds(aligned(2 * line + origin // share, 256), 256),
                    pl.ds(aligned(origin % share, 128), 128),
                ],
            )

    from_y("wy_up", down)
    block = wo.at[pl.ds(aligned(2 * down, 256), 256), :]
    send("wy_on_up", block, block, at(yy=up))
    from_y("wy_down", up)
    block = wo.at[pl.ds(aligned(2 * up + 1, 256), 256), :]
    send("wy_on_down", block, block, at(yy=down))

    relay_x(0)

    relay_x(1)

    def product(index):
        return dot(gated[index], wo[pl.ds(aligned(index, 256), 256), :])

    for copy in sent[:early]:
        copy.wait_send()

    @pl.when(c == holder)
    def _():
        for copy in emb_copies():
            copy.wait_send()
        for _, copy in emb_relays():
            copy.wait_send()

    @pl.when(moves)
    def _():
        swap_copy().wait_send()

    receive("wy_on_up", wo.at[pl.ds(aligned(2 * opposite, 256), 256), :])
    receive("wy_on_down", wo.at[pl.ds(aligned(2 * opposite + 1, 256), 256), :])
    total[...] = product(j)
    total[...] += product(left_j)
    for part in range(2):
        receive("g_on_right%d" % part, quarter(across_j, 2 * part))
        receive("g_on_left%d" % part, quarter(across_j, 2 * part + 1))
        send("m_across%d" % part, half(across_j, part), half(across_j, part), mate)
        if part == 0:
            total[...] += product(right_j)
    receive("g_mate0", half(mate_j, 0))
    receive("g_mate1", half(mate_j, 1))
    total[...] += product(mate_j)
    for name, place in (("left", left), ("right", right), ("across", across)):
        index = place * NC + 1 - c
        if name == "across":
            total[...] += product(across_j)
        receive("m_" + name + "0", half(index, 0))
        receive("m_" + name + "1", half(index, 1))
        if name == "across":
            out_ref[...] = (total[...] + product(index)).astype(bf16)
        else:
            total[...] += product(index)

    for copy in sent[early:]:
        copy.wait_send()


SEMAPHORES = 240


def body(
    tokens,
    embedding,
    norm_gain,
    in_weight,
    short_taps,
    decay_rates,
    residue,
    skip_weight,
    out_weight,
):
    whole = pl.BlockSpec(memory_space=pltpu.VMEM)
    outside = pl.BlockSpec(memory_space=pl.ANY)
    vm = pltpu.VMEM
    return pl.pallas_call(
        kernel,
        out_shape=jax.ShapeDtypeStruct((512, 512), bf16),
        in_specs=[outside] * 9,
        out_specs=whole,
        scratch_shapes=[
            vm((4, 128), jnp.int32),
            vm((32, 128), f32),
            vm((1, 256), f32),
            vm((3, 7, 256), f32),
            vm((16, 16), f32),
            vm((16, 16), f32),
            vm((3, 128, 256), bf16),
            vm((512, 512), bf16),
            vm((3, 256, 128), bf16),
            vm((NY, 3, 64, 128), bf16),
            vm((NX, 512, 128), bf16),
            vm((512, 512), bf16),
            vm((NX * NC, 1, 512), f32),
            vm((NZ, 16, 512), bf16),
            vm((NZ, 16, 256), bf16),
            vm((NZ, 16, 512), bf16),
            vm((NZ, 16, 256), bf16),
            vm((16, 512), f32),
            vm((16, 256), f32),
            vm((24, 512), f32),
            vm((NY, NZ, 4, 128), jnp.int32),
            vm((128, 128), f32),
            vm((128, 128), f32),
            vm((64, 128, 256), bf16),
            vm((3, 1088, 128), f32),
            vm((3, 7, 8, 128), f32),
            vm((1024, 128), f32),
            vm((1024, 128), f32),
            vm((128, 1024), f32),
            vm((1024, 128), f32),
            vm((1024, 128), bf16),
            vm((NY * NZ, 32, 128), bf16),
            vm((NX * NC, 512, 256), bf16),
            vm((2048, 512), bf16),
            vm((512, 512), f32),
            pltpu.SemaphoreType.DMA((8,)),
            pltpu.SemaphoreType.DMA((SEMAPHORES,)),
            pltpu.SemaphoreType.DMA((SEMAPHORES,)),
        ],
        compiler_params=pltpu.CompilerParams(
            collective_id=0, has_side_effects=True, vmem_limit_bytes=60 * 1024 * 1024
        ),
    )(
        tokens.reshape(4, 128),
        norm_gain.reshape(32, 128),
        skip_weight.reshape(1, 256),
        short_taps.transpose(1, 0, 2),
        decay_rates,
        residue,
        in_weight.transpose(1, 0, 2),
        embedding,
        out_weight,
    )


def solution(mesh):
    placed = (
        P("ctx"),
        P(None, "fsdp"),
        P(),
        P("ctx", None, "fsdp"),
        P(None, None, "fsdp"),
        P(None, "fsdp"),
        P(None, "fsdp"),
        P("fsdp"),
        P("fsdp", "ctx"),
    )
    return jax.shard_map(
        body, mesh=mesh, in_specs=placed, out_specs=P("ctx", "fsdp"), check_vma=False
    )
```
